512 devices in a mesh: space: 128 (over z, y, core), code: 4 (over x).
Axes of the slice: x: 4, y: 4, z: 16, core: 2. Of those that a mesh axis runs over, the one named last changes fastest.
Arguments:
- geometry: bfloat16 [4, 6, 1048576], P('code', None, 'space'), as said below
- codebook: bfloat16 [48, 4096], P(None, 'code'), may hold values from -3 to 3
- word_ids: int32 [1048576], P('space'), may hold values from 0 to 4095
- residual: bfloat16 [12, 1048576], P(None, 'space'), may hold values from -2 to 2
- send_list: int32 [4, 128, 128], P('code', 'space'), may hold values from 0 to 63
- tile_list: int32 [4, 1024, 4], P('code', 'space'), may hold values from 0 to 127, as said below
- rays: float32 [4, 3, 262144], P('code', None, 'space'), as said below
- target: int32 [4, 3, 262144], P('code', None, 'space'), may hold values from 0 to 255
Outputs:
- rendered: float32 [4, 3, 262144], P('code', None, 'space')
- foot_grad: float32 [4, 6, 1048576], P('code', None, 'space')
- resid_grad: float32 [12, 1048576], P(None, 'space')
- code_grad: float32 [48, 4096], P(None, 'code')
The draws below stay inside these ranges and needn't reach their ends.
Inputs may be any that keep to these rules, and one draw needn't show every extreme that they name: `tile_list`: each row names 4 different owners. `geometry`: conics are positive definite, |b| at most 0.6 sqrt(a c); opacities are positive and at most 0.5. `rays`: every ray has length 0.8 to 1.2; directions may point anywhere.
All inputs are finite; a program needn't handle non-finite values.
Results may differ from the reference program's by a relative error of at most 0.0021.
Values may be sent and summed in bfloat16 or wider, within the bound.
A program may use at most 64 MiB of HBM per device.

```python
import math
import jax
import jax.numpy as jnp
import numpy as np
from jax import lax

WORDS = 4096
COEF = 48
RESID = 12
BLOCK = 128
LIST = 4
SIDE = 16
B_DEV = 64
TILE_PIX = 256
VIEWS = 4
SPLATS = 1048576
TILES = 1024
PIXELS = 262144
N_SPACE = 128


def draw_geometry(key, part):
    key = jax.random.fold_in(key, 11)
    random_key_list = jax.random.split(key, 8)
    dimension_sizes = (VIEWS, SPLATS)
    center_u = jax.random.uniform(random_key_list[0], dimension_sizes, minval=-12.0, maxval=12.0)
    center_v = jax.random.uniform(random_key_list[1], dimension_sizes, minval=-12.0, maxval=12.0)
    sigma_u = jnp.exp(jax.random.uniform(random_key_list[2], dimension_sizes, minval=math.log(2.0), maxval=math.log(12.0)))
    sigma_v = jnp.exp(jax.random.uniform(random_key_list[3], dimension_sizes, minval=math.log(2.0), maxval=math.log(12.0)))
    correlation = jax.random.uniform(random_key_list[4], dimension_sizes, minval=-0.6, maxval=0.6)
    scale = 1.0 / (1.0 - correlation * correlation)
    conic_a = scale / (sigma_u * sigma_u)
    conic_c = scale / (sigma_v * sigma_v)
    conic_b = -correlation * scale / (sigma_u * sigma_v)
    dim_splats = jnp.exp(jax.random.uniform(random_key_list[5], dimension_sizes, minval=math.log(0.001), maxval=math.log(0.02)))
    sudden_spike = jax.random.randint(random_key_list[6], dimension_sizes, 0, 50) == 0
    bright_splats = jax.random.uniform(random_key_list[7], dimension_sizes, minval=0.2, maxval=0.5)
    alpha_value = jnp.where(sudden_spike, bright_splats, dim_splats)
    stacked = jnp.stack([center_u, center_v, conic_a, conic_b, conic_c, alpha_value], axis=1)
    return stacked.astype(jnp.bfloat16)


def draw_rays(key, part):
    key = jax.random.fold_in(key, 23)
    random_key_list = jax.random.split(key, 3)
    dimension_sizes = (VIEWS, PIXELS)
    turn = jax.random.uniform(random_key_list[0], dimension_sizes, minval=-math.pi, maxval=math.pi)
    height = jax.random.uniform(random_key_list[1], dimension_sizes, minval=-1.0, maxval=1.0)
    length = jax.random.uniform(random_key_list[2], dimension_sizes, minval=0.8, maxval=1.2)
    spread = jnp.sqrt(jnp.maximum(1.0 - height * height, 0.0))
    across = length * spread * jnp.cos(turn)
    upward = length * spread * jnp.sin(turn)
    depth = length * height
    return jnp.stack([across, upward, depth], axis=1).astype(jnp.float32)


def draw_tile_list(key, part):
    key = jax.random.fold_in(key, 37)
    random_key_list = jax.random.split(key, VIEWS * TILES)

    def pick_row(row_key):
        return jax.random.permutation(row_key, N_SPACE)[:LIST]
    chosen = jax.vmap(pick_row)(random_key_list)
    return chosen.reshape(VIEWS, TILES, LIST).astype(jnp.int32)


def plant(array, stream_key, least, largest):
    longest = array.shape.index(max(array.shape))
    spots = []
    for shift in (0, 1):
        where = [jax.random.randint(jax.random.fold_in(stream_key, axis), (), 0, length) for axis, length in enumerate(array.shape)]
        where[longest] = (where[longest] + shift) % array.shape[longest]
        spots.append(tuple(where))
    return array.at[spots[0]].set(least).at[spots[1]].set(largest)


def block_scale(rng, extent, cuts, least, high):
    loudness = 1.0
    for position, blocks in cuts:
        steps = jax.random.uniform(jax.random.fold_in(jax.random.fold_in(rng, 6), position), (blocks,), jnp.float32, least / len(cuts), high / len(cuts))
        loudness = loudness * jnp.repeat(jnp.exp(steps), extent[position] // blocks).reshape((-1,) + (1,) * (len(extent) - 1 - position))
    return loudness


def rank_bounds(amount, slope):
    loads = [(1 << 20) // math.isqrt(grade ** slope) + 1 for grade in range(1, amount + 1)]
    width = 1 + sum(loads) // (1 << 30)
    return np.cumsum(np.array([max(1, weight // width) for weight in loads]))


def ranked(rng, extent, count, slope):
    listing = rank_bounds(count, slope)
    pick = jax.random.randint(jax.random.fold_in(rng, 1), extent, 0, int(listing[count - 1]))
    grade = jnp.searchsorted(jnp.asarray(listing, jnp.int32), pick, side="right")
    return jax.random.permutation(jax.random.fold_in(rng, 2), count)[grade].astype(jnp.int32)


def bell_draw(rng, extent, scale, most, shards=(), kind=jnp.bfloat16):
    drawn = jax.random.normal(rng, extent, jnp.float32) * scale
    if len(shards) > 0:
        drawn = block_scale(rng, extent, shards, -0.22, 0.18) * drawn
    return jnp.clip(drawn, min=-most, max=most).astype(kind)


def setup_inputs(seed: int = 0) -> dict:
    seeds = jax.random.split(jax.random.key(seed), 9)
    return {
        "geometry": draw_geometry(jax.random.fold_in(seeds[8], 71), 0),
        "codebook": bell_draw(seeds[1], (COEF, WORDS), 0.5, 3.0, ((1, 4),)),
        "word_ids": plant(ranked(seeds[2], (SPLATS,), WORDS, 1), jax.random.fold_in(seeds[2], 3), 0, WORDS - 1).astype(jnp.int32),
        "residual": bell_draw(seeds[3], (RESID, SPLATS), 0.3, 2.0, ((1, 128),)),
        "send_list": plant(jax.random.randint(seeds[4], (VIEWS, N_SPACE, N_SPACE), 0, B_DEV), jax.random.fold_in(seeds[4], 1), 0, B_DEV - 1).astype(jnp.int32),
        "tile_list": draw_tile_list(jax.random.fold_in(seeds[8], 71), 0),
        "rays": draw_rays(jax.random.fold_in(seeds[8], 71), 0),
        "target": plant(jax.random.randint(seeds[7], (VIEWS, 3, PIXELS), 0, 256), jax.random.fold_in(seeds[7], 1), 0, 255).astype(jnp.int32),
    }


band_zero = 0.28209479177387814
band_one = 0.4886025119029199
band_two = (1.0925484305920792, -1.0925484305920792, 0.31539156525252005, -1.0925484305920792, 0.5462742152960396)
band_three = (-0.5900435899266435, 2.890611442640554, -0.4570457994644658, 0.3731763325901154, -0.4570457994644658, 1.445305721320277, -0.5900435899266435)

def harmonics(direction):
    length = jnp.sqrt(lax.optimization_barrier(jnp.sum(direction * direction, axis=0)))
    coord_x = direction[0] / length
    coord_y = direction[1] / length
    coord_z = direction[2] / length
    square_x = coord_x * coord_x
    square_y = coord_y * coord_y
    square_z = coord_z * coord_z
    entries = [band_zero * jnp.ones_like(coord_x), -band_one * coord_y, band_one * coord_z, -band_one * coord_x, band_two[0] * coord_x * coord_y, band_two[1] * coord_y * coord_z, band_two[2] * (2.0 * square_z - square_x - square_y), band_two[3] * coord_x * coord_z, band_two[4] * (square_x - square_y), band_three[0] * coord_y * (3.0 * square_x - square_y), band_three[1] * coord_x * coord_y * coord_z, band_three[2] * coord_y * (4.0 * square_z - square_x - square_y), band_three[3] * coord_z * (2.0 * square_z - 3.0 * square_x - 3.0 * square_y), band_three[4] * coord_x * (4.0 * square_z - square_x - square_y), band_three[5] * coord_z * (square_x - square_y), band_three[6] * coord_x * (square_x - 3.0 * square_y)]
    return jnp.stack(entries)

def pixel_offsets(side):
    pixel_index = jnp.arange(side * side, dtype=jnp.int32)
    offset_u = (pixel_index % side).astype(jnp.float32) - (side - 1) * 0.5
    offset_v = (pixel_index // side).astype(jnp.float32) - (side - 1) * 0.5
    return jnp.stack([offset_u, offset_v])

def composite(footprint, palette, harmonic_rows, offsets):
    delta_u = offsets[0][:, None] - footprint[0][None, :]
    delta_v = offsets[1][:, None] - footprint[1][None, :]
    exponent = -0.5 * (footprint[2] * delta_u * delta_u + 2.0 * footprint[3] * delta_u * delta_v + footprint[4] * delta_v * delta_v)
    absorb = footprint[5] * jnp.exp(exponent)
    keep_log = jnp.log1p(-absorb)
    before = jnp.cumsum(keep_log, axis=1) - keep_log
    weight = jnp.exp(before) * absorb
    mixed = jnp.dot(weight, palette.T, precision=lax.Precision.HIGHEST)
    mixed = mixed.reshape(mixed.shape[0], 16, 3)
    return jnp.einsum('kp,pkc->cp', harmonic_rows, mixed, precision=lax.Precision.HIGHEST) + 0.5 * lax.optimization_barrier(jnp.sum(weight, axis=1))[None, :]

def render_group(footprint, palette, harmonic_rows, destination_group, offsets):

    def forward(foot_all, palette_group):
        return jax.vmap(composite, in_axes=(0, 0, 0, None))(foot_all, palette_group, harmonic_rows, offsets)
    images, pullback = jax.vjp(forward, footprint, palette)
    grad_foot, grad_palette = pullback(images - destination_group)
    return (images, grad_foot, grad_palette)

def decode(codebook, word_ids, residual):
    looked = jnp.take(codebook, word_ids, axis=1).astype(jnp.float32)
    upper = looked[:RESID] + residual.astype(jnp.float32)
    decoded = jnp.concatenate([upper, looked[RESID:]], axis=0).astype(jnp.bfloat16)
    return lax.optimization_barrier(decoded)

def reference(geometry, codebook, word_ids, residual, send_list, tile_list, rays, target):
    views = geometry.shape[0]
    n_space = send_list.shape[1]
    tiles = tile_list.shape[1]
    per_dev = tiles // n_space
    list_width = LIST * BLOCK
    palette_all = decode(codebook, word_ids, residual).astype(jnp.float32)
    footprint_all = geometry.astype(jnp.float32)
    harmonic_all = jax.vmap(harmonics)(rays)
    harmonic_tiles = harmonic_all.reshape(views, 16, tiles, TILE_PIX).transpose(0, 2, 1, 3).reshape(views * tiles, 16, TILE_PIX)
    target_tiles = (target.astype(jnp.float32) / 255.0).reshape(views, 3, tiles, TILE_PIX).transpose(0, 2, 1, 3).reshape(views * tiles, 3, TILE_PIX)
    owner_dev = jnp.arange(tiles, dtype=jnp.int32) // per_dev
    view_index = jnp.arange(views, dtype=jnp.int32)
    chosen = send_list[view_index[:, None, None], tile_list, owner_dev[None, :, None]]
    members = ((tile_list * B_DEV + chosen) * BLOCK)[..., None] + jnp.arange(BLOCK, dtype=jnp.int32)
    members = members.reshape(views * tiles, list_width).astype(jnp.int32)
    view_of = jnp.repeat(view_index, tiles)
    tile_total = views * tiles
    per_step = math.gcd(tile_total, 8)
    step_count = tile_total // per_step
    offsets = pixel_offsets(SIDE)

    def render_step(running, inputs):
        foot_grad, palette_grad = running
        member_group, view_group, harmonic_group, destination_group = inputs
        footprint = jnp.moveaxis(footprint_all[view_group[:, None], :, member_group], 2, 1)
        palette = jnp.moveaxis(palette_all[:, member_group], 0, 1)
        images, grad_foot, grad_palette = render_group(footprint, palette, harmonic_group, destination_group, offsets)
        foot_grad = foot_grad.at[view_group[:, None], :, member_group].add(jnp.moveaxis(grad_foot, 1, 2))
        palette_grad = palette_grad.at[:, member_group].add(jnp.moveaxis(grad_palette, 0, 1))
        return ((foot_grad, palette_grad), images)
    start = (jnp.zeros(footprint_all.shape, jnp.float32), jnp.zeros(palette_all.shape, jnp.float32))
    (foot_grad, palette_grad), images = lax.scan(render_step, start, (members.reshape(step_count, per_step, list_width), view_of.reshape(step_count, per_step), harmonic_tiles.reshape(step_count, per_step, 16, TILE_PIX), target_tiles.reshape(step_count, per_step, 3, TILE_PIX)))
    rendered = images.reshape(views, tiles, 3, TILE_PIX).transpose(0, 2, 1, 3).reshape(views, 3, tiles * TILE_PIX)
    resid_grad = palette_grad[:RESID]
    code_grad = jax.ops.segment_sum(palette_grad.T, word_ids, num_segments=WORDS).T
    return (rendered, foot_grad, resid_grad, code_grad)
```

```python
import functools
import math

import jax
import jax.numpy as jnp
import numpy as np
from jax import lax
from jax.experimental import pallas as pl
from jax.experimental.pallas import tpu as pltpu
from jax.sharding import PartitionSpec as P

WORDS = 4096
COEF = 48
RESID = 12
GEO = 6
BLOCK = 128
LIST = 4
SIDE = 16
TILE_PIX = 256
WIDTH = LIST * BLOCK
GROUPS = 4
GWORDS = WORDS // GROUPS
ROWS_OUT = 24
ROWS_BACK = 32
LOG2E = 1.4426950408889634
F32 = jnp.float32
BF16 = jnp.bfloat16

band_zero = 0.28209479177387814
band_one = 0.4886025119029199
band_two = (
    1.0925484305920792,
    -1.0925484305920792,
    0.31539156525252005,
    -1.0925484305920792,
    0.5462742152960396,
)
band_three = (
    -0.5900435899266435,
    2.890611442640554,
    -0.4570457994644658,
    0.3731763325901154,
    -0.4570457994644658,
    1.445305721320277,
    -0.5900435899266435,
)


def harmonic_rows(ray_x, ray_y, ray_z):
    length = jnp.sqrt(ray_x * ray_x + ray_y * ray_y + ray_z * ray_z)
    x = ray_x / length
    y = ray_y / length
    z = ray_z / length
    xx, yy, zz = x * x, y * y, z * z
    return [
        band_zero * jnp.ones_like(x),
        -band_one * y,
        band_one * z,
        -band_one * x,
        band_two[0] * x * y,
        band_two[1] * y * z,
        band_two[2] * (2.0 * zz - xx - yy),
        band_two[3] * x * z,
        band_two[4] * (xx - yy),
        band_three[0] * y * (3.0 * xx - yy),
        band_three[1] * x * y * z,
        band_three[2] * y * (4.0 * zz - xx - yy),
        band_three[3] * z * (2.0 * zz - 3.0 * xx - 3.0 * yy),
        band_three[4] * x * (4.0 * zz - xx - yy),
        band_three[5] * z * (xx - yy),
        band_three[6] * x * (xx - 3.0 * yy),
    ]


def nn(a, b):
    return lax.dot_general(a, b, (((1,), (0,)), ((), ())), preferred_element_type=F32)


def nt(a, b):
    return lax.dot_general(a, b, (((1,), (1,)), ((), ())), preferred_element_type=F32)


def tn(a, b):
    return lax.dot_general(a, b, (((0,), (0,)), ((), ())), preferred_element_type=F32)


def pack_kernel(send_ref, geo_ref, word_ref, resid_ref, out_ref, blocks_ref):
    blocks = blocks_ref.shape[0]

    def build(b, carry):
        lanes = pl.ds(pl.multiple_of(b * BLOCK, BLOCK), BLOCK)
        ids = word_ref[pl.ds(b, 1), :]
        high = (ids >> 8).astype(F32)
        low = (ids & 255).astype(F32)
        geo = geo_ref[:, lanes].astype(F32)
        resid = resid_ref[:, lanes].astype(F32)
        whole = jnp.concatenate([geo, high, low, resid, jnp.zeros((4, BLOCK), F32)], axis=0)
        blocks_ref[b] = whole.astype(BF16)
        return carry

    lax.fori_loop(0, blocks, build, 0, unroll=4)

    def copy(d, carry):
        out_ref[d] = blocks_ref[send_ref[d]]
        return carry

    lax.fori_loop(0, out_ref.shape[0], copy, 0, unroll=8)


def pack(sent, geo, words, resid):
    blocks = words.shape[0]
    return pl.pallas_call(
        pack_kernel,
        out_shape=jax.ShapeDtypeStruct((sent.shape[0], ROWS_OUT, BLOCK), BF16),
        in_specs=[pl.BlockSpec(memory_space=pltpu.SMEM)]
        + [pl.BlockSpec(memory_space=pltpu.VMEM)] * 3,
        out_specs=pl.BlockSpec(memory_space=pltpu.VMEM),
        scratch_shapes=[pltpu.VMEM((blocks, ROWS_OUT, BLOCK), BF16)],
        name="pack",
    )(sent, geo, words, resid)


def constants():
    perm = np.zeros((56, 56), np.float32)
    for j in range(16):
        for ch in range(3):
            perm[ch * 16 + j, 3 * j + ch] = 1.0
    perm[48, 48] = 1.0
    spread = np.zeros((256, 56), np.float32)
    for j in range(16):
        for g in range(GROUPS):
            for ch in range(3):
                spread[j * 16 + g * 3 + ch, ch * 16 + j] = 1.0
    return jnp.asarray(perm, BF16), jnp.asarray(spread, BF16)


def render_kernel(
    tile_ref,
    recv_ref,
    book_ref,
    rays_ref,
    target_ref,
    perm_ref,
    spread_ref,
    img_ref,
    back_ref,
    acc_ref,
    words_ref,
    harm_ref,
    tri_ref,
    tris_ref,
    hot_ref,
    e_ref,
    log_ref,
    cum_ref,
    wp_ref,
    wb_ref,
    wl_ref,
    g_ref,
    wg_ref,
):
    tiles = tile_ref.shape[0]
    row_i = lax.broadcasted_iota(jnp.int32, (WIDTH, WIDTH), 0)
    col_i = lax.broadcasted_iota(jnp.int32, (WIDTH, WIDTH), 1)
    tri_ref[...] = jnp.where(row_i < col_i, 1.0, 0.0).astype(BF16)
    tris_ref[...] = jnp.where(row_i > col_i, 1.0, 0.0).astype(BF16)
    acc_ref[...] = jnp.zeros_like(acc_ref)
    words_ref[...] = jnp.zeros_like(words_ref)
    for j, row in enumerate(harmonic_rows(rays_ref[0:1, :], rays_ref[1:2, :], rays_ref[2:3, :])):
        harm_ref[j : j + 1, :] = row
    u = lax.broadcasted_iota(jnp.int32, (SIDE, WIDTH), 0).astype(F32) - (SIDE - 1) * 0.5
    half = WIDTH // 2

    def tile_step(t, carry):
        pix = pl.ds(pl.multiple_of(t * TILE_PIX, TILE_PIX), TILE_PIX)
        src = [tile_ref[t, l] for l in range(LIST)]
        msg = jnp.concatenate([recv_ref[src[l]] for l in range(LIST)], axis=1).astype(F32)
        cu, cv, ca, cb, cc, op = [msg[i : i + 1] for i in range(GEO)]
        high, low = msg[6:7], msg[7:8]
        resid = msg[8:24]
        du = u - cu
        base_u = (-0.5 * LOG2E) * ca * du * du
        cross = (-LOG2E) * cb * du
        curve = (-0.5 * LOG2E) * cc
        for v in range(SIDE):
            rows = slice(v * SIDE, (v + 1) * SIDE)
            dv = (v - (SIDE - 1) * 0.5) - cv
            e = jnp.exp2(base_u + cross * dv + curve * dv * dv)
            lg = jnp.log2(1.0 - op * e)
            lg_hi = lg.astype(BF16)
            e_ref[rows, :] = e
            log_ref[rows, :] = lg_hi
            log_ref[TILE_PIX + v * SIDE : TILE_PIX + (v + 1) * SIDE, :] = (
                lg - lg_hi.astype(F32)
            ).astype(BF16)
        cum_ref[:, :half] = nn(log_ref[:, :half], tri_ref[:half, :half])
        cum_ref[:, half:] = nn(log_ref[...], tri_ref[:, half:])
        for v in range(SIDE):
            rows = slice(v * SIDE, (v + 1) * SIDE)
            cum = cum_ref[rows, :] + cum_ref[TILE_PIX + v * SIDE : TILE_PIX + (v + 1) * SIDE, :]
            wp = jnp.exp2(cum) * e_ref[rows, :]
            wp_ref[rows, :] = wp
            weight = wp * op
            weight_hi = weight.astype(BF16)
            wb_ref[rows, :] = weight_hi
            wl_ref[rows, :] = (weight - weight_hi.astype(F32)).astype(BF16)
        group = jnp.floor(high * 0.25)
        part = high - 4.0 * group
        word_row = lax.broadcasted_iota(jnp.int32, (256, 1), 0).astype(F32)
        for c in range(4):
            key = jnp.where(part == float(c), low, -1.0)
            hot_ref[c * 256 : (c + 1) * 256, :] = jnp.where(word_row == key, 1.0, 0.0).astype(BF16)
        looked_all = nn(book_ref[...], hot_ref[...])
        looked = jnp.where(group == 0.0, looked_all[:COEF], 0.0)
        for g in range(1, GROUPS):
            looked = jnp.where(group == float(g), looked_all[g * COEF : (g + 1) * COEF], looked)
        eight = lax.broadcasted_iota(jnp.int32, (8, WIDTH), 0)
        palette = jnp.concatenate(
            [looked[:16] + resid, looked[16:], jnp.where(eight == 0, 0.5, 0.0)], axis=0
        ).astype(BF16)
        palette = nn(perm_ref[...], palette).astype(BF16)
        mixed = nt(palette, wb_ref[...]) + nt(palette, wl_ref[...])
        harm = harm_ref[:, pix]
        image = jnp.concatenate(
            [
                jnp.sum(harm * mixed[ch * 16 : (ch + 1) * 16], axis=0, keepdims=True)
                + mixed[48:49]
                for ch in range(3)
            ],
            axis=0,
        )
        img_ref[:, pix] = image
        off = image - target_ref[:, pix].astype(F32) / 255.0
        total = off[0:1] + off[1:2] + off[2:3]
        pix8 = lax.broadcasted_iota(jnp.int32, (8, TILE_PIX), 0)
        grad = jnp.concatenate(
            [harm * off[ch : ch + 1] for ch in range(3)] + [jnp.where(pix8 == 0, total, 0.0)],
            axis=0,
        )
        grad_hi = grad.astype(BF16)
        grad_lo = (grad - grad_hi.astype(F32)).astype(BF16)
        g_ref[...] = tn(grad_hi, palette) + tn(grad_lo, palette)
        color = nn(grad_hi, wb_ref[...]) + nn(grad_lo, wb_ref[...]) + nn(grad_hi, wl_ref[...])
        spread = nn(spread_ref[...], color.astype(BF16))
        sixteen = lax.broadcasted_iota(jnp.int32, (16, 1), 0)
        row_group = jnp.where(
            sixteen < 3, 0.0, jnp.where(sixteen < 6, 1.0, jnp.where(sixteen < 9, 2.0, 3.0))
        )
        mask = jnp.where(row_group == group, 1.0, 0.0)
        masked = jnp.concatenate(
            [(spread[i * 16 : (i + 1) * 16] * mask).astype(BF16) for i in range(16)], axis=0
        )
        words_ref[...] += nt(masked, hot_ref[...])
        for v in range(SIDE):
            rows = slice(v * SIDE, (v + 1) * SIDE)
            wg_ref[rows, :] = (wp_ref[rows, :] * g_ref[rows, :] * op).astype(BF16)
        cum_ref[:TILE_PIX, half:] = nn(wg_ref[:, half:], tris_ref[half:, half:])
        cum_ref[:TILE_PIX, :half] = nn(wg_ref[...], tris_ref[:, :half])
        s_zero = jnp.zeros((SIDE, WIDTH), F32)
        s_one = jnp.zeros((SIDE, WIDTH), F32)
        s_two = jnp.zeros((SIDE, WIDTH), F32)
        for v in range(SIDE):
            rows = slice(v * SIDE, (v + 1) * SIDE)
            e = e_ref[rows, :]
            p = wp_ref[rows, :] * g_ref[rows, :] - cum_ref[rows, :] * (e / (1.0 - op * e))
            dv = (v - (SIDE - 1) * 0.5) - cv
            pd = p * dv
            s_zero = s_zero + p
            s_one = s_one + pd
            s_two = s_two + pd * dv
        m_zero = jnp.sum(s_zero, axis=0, keepdims=True)
        m_u = jnp.sum(s_zero * du, axis=0, keepdims=True)
        m_uu = jnp.sum(s_zero * du * du, axis=0, keepdims=True)
        m_v = jnp.sum(s_one, axis=0, keepdims=True)
        m_uv = jnp.sum(s_one * du, axis=0, keepdims=True)
        m_vv = jnp.sum(s_two, axis=0, keepdims=True)
        zero = jnp.zeros((1, WIDTH), F32)
        rows_back = jnp.concatenate(
            [
                color[0:4],
                color[16:20],
                color[32:36],
                op * (ca * m_u + cb * m_v),
                op * (cb * m_u + cc * m_v),
                -0.5 * op * m_uu,
                -op * m_uv,
                -0.5 * op * m_vv,
                m_zero,
                zero,
                zero,
                zero,
                zero,
                zero,
                zero,
            ],
            axis=0,
        )
        for l in range(LIST):
            acc_ref[src[l]] += rows_back[:, l * BLOCK : (l + 1) * BLOCK]
        return carry

    lax.fori_loop(0, tiles, tile_step, 0)

    def finish(j, carry):
        for lane in range(8):
            d = j * 8 + lane
            back_ref[d, 0:16, :] = acc_ref[d, 0:16, :].astype(BF16)
            word = words_ref[
                pl.ds(pl.multiple_of(j * 16, 16), 16), lane * BLOCK : (lane + 1) * BLOCK
            ]
            shifted = pltpu.roll(acc_ref[d, 16:24, :], 4, 0)
            word = jnp.concatenate([word[:8], word[8:] + shifted], axis=0)
            back_ref[d, 16:32, :] = word.astype(BF16)
        return carry

    lax.fori_loop(0, 16, finish, 0)


def render(tile_rows, recv, book, rays, target):
    perm, spread = constants()
    pixels = rays.shape[1]
    n = recv.shape[0]
    return pl.pallas_call(
        render_kernel,
        out_shape=(
            jax.ShapeDtypeStruct((3, pixels), F32),
            jax.ShapeDtypeStruct((n, ROWS_BACK, BLOCK), BF16),
        ),
        in_specs=[pl.BlockSpec(memory_space=pltpu.SMEM)]
        + [pl.BlockSpec(memory_space=pltpu.VMEM)] * 6,
        out_specs=(pl.BlockSpec(memory_space=pltpu.VMEM),) * 2,
        scratch_shapes=[
            pltpu.VMEM((n, 24, BLOCK), F32),
            pltpu.VMEM((256, GWORDS), F32),
            pltpu.VMEM((16, pixels), F32),
            pltpu.VMEM((WIDTH, WIDTH), BF16),
            pltpu.VMEM((WIDTH, WIDTH), BF16),
            pltpu.VMEM((GWORDS, WIDTH), BF16),
            pltpu.VMEM((TILE_PIX, WIDTH), F32),
            pltpu.VMEM((2 * TILE_PIX, WIDTH), BF16),
            pltpu.VMEM((2 * TILE_PIX, WIDTH), F32),
            pltpu.VMEM((TILE_PIX, WIDTH), F32),
            pltpu.VMEM((TILE_PIX, WIDTH), BF16),
            pltpu.VMEM((TILE_PIX, WIDTH), BF16),
            pltpu.VMEM((TILE_PIX, WIDTH), F32),
            pltpu.VMEM((TILE_PIX, WIDTH), BF16),
        ],
        compiler_params=pltpu.CompilerParams(vmem_limit_bytes=48 * 2**20),
        name="render",
    )(tile_rows, recv, book, rays, target, perm, spread)


def owner_kernel(send_ref, back_ref, foot_ref, resid_ref, word_ref, own_ref):
    blocks = own_ref.shape[0]
    own_ref[...] = jnp.zeros_like(own_ref)

    def add(d, words):
        part = back_ref[d].astype(F32)
        b = send_ref[d]
        own_ref[b, 0:16, :] += part[0:16]
        own_ref[b, 16:24, :] += part[24:32]
        return words + part[16:32]

    word_ref[...] = lax.fori_loop(
        0, back_ref.shape[0], add, jnp.zeros((16, BLOCK), F32), unroll=4
    )

    def write(b, carry):
        lanes = pl.ds(pl.multiple_of(b * BLOCK, BLOCK), BLOCK)
        own = own_ref[b]
        resid_ref[:, lanes] = own[0:16].astype(BF16)
        foot_ref[:, lanes] = jnp.concatenate([own[12:16], own[20:22]], axis=0)
        return carry

    lax.fori_loop(0, blocks, write, 0, unroll=4)


def owner_sum(sent, back, blocks):
    return pl.pallas_call(
        owner_kernel,
        out_shape=(
            jax.ShapeDtypeStruct((GEO, blocks * BLOCK), F32),
            jax.ShapeDtypeStruct((16, blocks * BLOCK), BF16),
            jax.ShapeDtypeStruct((16, BLOCK), F32),
        ),
        in_specs=[
            pl.BlockSpec(memory_space=pltpu.SMEM),
            pl.BlockSpec(memory_space=pltpu.VMEM),
        ],
        out_specs=(pl.BlockSpec(memory_space=pltpu.VMEM),) * 3,
        scratch_shapes=[pltpu.VMEM((blocks, 24, BLOCK), F32)],
        name="owner_sum",
    )(sent, back)


def on_device(geometry, codebook, word_ids, residual, send_list, tile_list, rays, target):
    blocks = word_ids.shape[0] // BLOCK
    n_space = lax.axis_size("space")
    sent = send_list[0, 0]
    message = pack(sent, geometry[0], word_ids.reshape(blocks, BLOCK), residual)
    book = lax.all_gather(codebook, "code", axis=0, tiled=True)
    recv = lax.all_to_all(message, "space", split_axis=0, concat_axis=0, tiled=True)
    image, back = render(tile_list[0], recv, book, rays[0], target[0])
    returned = lax.all_to_all(back, "space", split_axis=0, concat_axis=0, tiled=True)
    foot, resid_part, word_part = owner_sum(sent, returned, blocks)
    resid_all = lax.all_gather(resid_part, "code", axis=0)
    resid_sum = jnp.sum(resid_all.astype(F32), axis=0)[:RESID]
    resid_grad = resid_sum.reshape(3, 4, -1).transpose(1, 0, 2).reshape(RESID, -1)
    word_x = lax.all_to_all(
        word_part[:12].reshape(GROUPS, 3 * BLOCK), "code", split_axis=0, concat_axis=0, tiled=True
    )
    word_sum = jnp.sum(word_x, axis=0)
    code = lax.all_gather(word_sum, "space", axis=0).reshape(16, 8, 3, BLOCK)
    code_grad = code.transpose(0, 2, 1, 3).reshape(COEF, GWORDS)
    return (image[None], foot[None], resid_grad, code_grad)


def solution(mesh):
    placed = (
        P("code", None, "space"),
        P(None, "code"),
        P("space"),
        P(None, "space"),
        P("code", "space", None),
        P("code", "space", None),
        P("code", None, "space"),
        P("code", None, "space"),
    )
    return jax.shard_map(
        on_device,
        mesh=mesh,
        in_specs=placed,
        out_specs=(
            P("code", None, "space"),
            P("code", None, "space"),
            P(None, "space"),
            P(None, "code"),
        ),
        check_vma=False,
    )
```

```python
import functools

import jax
import jax.numpy as jnp
import numpy as np
from jax import lax
from jax.experimental import pallas as pl
from jax.experimental.pallas import tpu as pltpu
from jax.sharding import PartitionSpec as P

WORDS = 4096
COEF = 48
RESID = 12
GEO = 6
BLOCK = 128
LIST = 4
SIDE = 16
TILE_PIX = 256
WIDTH = LIST * BLOCK
GROUPS = 4
GWORDS = WORDS // GROUPS
PAIRS_B = RESID // 2
PAIRS_T = 5
STAGE = 16
LOG2E = 1.4426950408889634
F32 = jnp.float32
BF16 = jnp.bfloat16
MESH = pl.DeviceIdType.MESH

band_zero = 0.28209479177387814
band_one = 0.4886025119029199
band_two = (
    1.0925484305920792,
    -1.0925484305920792,
    0.31539156525252005,
    -1.0925484305920792,
    0.5462742152960396,
)
band_three = (
    -0.5900435899266435,
    2.890611442640554,
    -0.4570457994644658,
    0.3731763325901154,
    -0.4570457994644658,
    1.445305721320277,
    -0.5900435899266435,
)


def harmonic_rows(ray_x, ray_y, ray_z):
    length = jnp.sqrt(ray_x * ray_x + ray_y * ray_y + ray_z * ray_z)
    x = ray_x / length
    y = ray_y / length
    z = ray_z / length
    xx, yy, zz = x * x, y * y, z * z
    return [
        band_zero * jnp.ones_like(x),
        -band_one * y,
        band_one * z,
        -band_one * x,
        band_two[0] * x * y,
        band_two[1] * y * z,
        band_two[2] * (2.0 * zz - xx - yy),
        band_two[3] * x * z,
        band_two[4] * (xx - yy),
        band_three[0] * y * (3.0 * xx - yy),
        band_three[1] * x * y * z,
        band_three[2] * y * (4.0 * zz - xx - yy),
        band_three[3] * z * (2.0 * zz - 3.0 * xx - 3.0 * yy),
        band_three[4] * x * (4.0 * zz - xx - yy),
        band_three[5] * z * (xx - yy),
        band_three[6] * x * (xx - 3.0 * yy),
    ]


def nn(a, b):
    return lax.dot_general(a, b, (((1,), (0,)), ((), ())), preferred_element_type=F32)


def nt(a, b):
    return lax.dot_general(a, b, (((1,), (1,)), ((), ())), preferred_element_type=F32)


def tn(a, b):
    return lax.dot_general(a, b, (((0,), (0,)), ((), ())), preferred_element_type=F32)


def greet(n_space, n_code):
    me, x = lax.axis_index("space"), lax.axis_index("code")
    barrier = pltpu.get_barrier_semaphore()

    def hello(k, carry):
        pl.semaphore_signal(
            barrier, inc=1, device_id={"space": lax.rem(me + k, n_space)}, device_id_type=MESH
        )
        return carry

    lax.fori_loop(1, n_space, hello, 0)
    for k in range(1, n_code):
        pl.semaphore_signal(
            barrier, inc=1, device_id={"code": lax.rem(x + k, n_code)}, device_id_type=MESH
        )
    return barrier


def to_space(n_space, fill, src, dst, send_sem, recv_sem):
    me = lax.axis_index("space")

    def one(d):
        if fill is not None:
            fill(d)
        pltpu.make_async_remote_copy(
            src_ref=src.at[d],
            dst_ref=dst.at[me],
            send_sem=send_sem,
            recv_sem=recv_sem,
            device_id={"space": d},
            device_id_type=MESH,
        ).start()

    def pair(k, carry):
        one(lax.rem(me + k, n_space))
        one(lax.rem(me + n_space - k, n_space))
        return carry

    lax.fori_loop(1, n_space // 2, pair, 0)
    one(lax.rem(me + n_space // 2, n_space))


def all_of(n_space, src, dst, send_sem, recv_sem):
    me = lax.axis_index("space")
    return pltpu.make_async_remote_copy(
        src_ref=src.at[pl.ds(0, n_space - 1)],
        dst_ref=dst.at[pl.ds(0, n_space - 1)],
        send_sem=send_sem,
        recv_sem=recv_sem,
        device_id={"space": lax.rem(me + 1, n_space)},
        device_id_type=MESH,
    )


def constants():
    perm = np.zeros((56, 56), np.float32)
    for j in range(16):
        for ch in range(3):
            perm[ch * 16 + j, 3 * j + ch] = 1.0
    perm[48, 48] = 1.0
    spread = np.zeros((128, COEF), np.float32)
    for k in range(COEF):
        spread[k // 3 * 8 + k % 3, k] = 1.0
    return jnp.asarray(perm, BF16), jnp.asarray(spread, BF16)


def put_rows(ref, row, value):
    ref[pl.ds(row, value.shape[0], stride=STAGE), :] = value


def get_rows(ref, row, count):
    return ref[pl.ds(row, count, stride=STAGE), :]


def step_kernel(
    n_space,
    n_code,
    send_ref,
    tile_ref,
    send_row_ref,
    tile_row_ref,
    geo_ref,
    word_ref,
    resid_ref,
    code_ref,
    rays_ref,
    target_ref,
    perm_ref,
    spread_ref,
    img_ref,
    foot_ref,
    resid_out_ref,
    code_out_ref,
    blocks_a,
    blocks_b,
    msg_a,
    msg_b,
    recv_a,
    recv_b,
    book_ref,
    e_ref,
    wp_ref,
    wb_ref,
    wl_ref,
    g_ref,
    hot_ref,
    look_ref,
    natural_ref,
    log_ref,
    cum_ref,
    wg_ref,
    tri_ref,
    tris_ref,
    harm_ref,
    words_ref,
    mine_ref,
    theirs_ref,
    wide_ref,
    grads_ref,
    stage_ref,
    stage_t_ref,
    msg_r,
    recv_r,
    msg_t,
    recv_t,
    own_ref,
    own_resid_ref,
    part_ref,
    line_ref,
    lines_ref,
    sems,
    code_send,
    code_recv,
    near_send,
    near_recv,
    far_send,
    far_recv,
):
    me, x = lax.axis_index("space"), lax.axis_index("code")
    tiles = tile_ref.shape[0]
    slots = tiles * LIST
    blocks = blocks_a.shape[0]
    half = WIDTH // 2
    barrier = greet(n_space, n_code)

    def lanes_of(i, width=BLOCK):
        return pl.ds(pl.multiple_of(i * width, width), width)

    def build(b, carry):
        ids = word_ref[pl.ds(b, 1), :]
        high = (ids >> 8).astype(F32)
        low = (ids & 255).astype(F32)
        geo = geo_ref[:, lanes_of(b)].astype(F32)
        blocks_a[b] = jnp.concatenate([geo, high, low], axis=0).astype(BF16)
        resid = resid_ref[:, lanes_of(b)].astype(F32)
        blocks_b[b] = jnp.concatenate(
            [resid[2 * i : 2 * i + 2] for i in range(PAIRS_B)], axis=1
        ).astype(BF16)
        return carry

    lax.fori_loop(0, blocks, build, 0, unroll=4)
    book_ref[x] = code_ref[...]
    pl.semaphore_wait(barrier, n_space + n_code - 2)

    def around(src, dst, first):
        copies = []
        for k in range(1, n_code):
            copies.append(
                pltpu.make_async_remote_copy(
                    src_ref=src(k),
                    dst_ref=dst(k),
                    send_sem=code_send.at[first + k - 1],
                    recv_sem=code_recv.at[first + k - 1],
                    device_id={"code": lax.rem(x + k, n_code)},
                    device_id_type=MESH,
                )
            )
            copies[-1].start()
        return copies

    def finish(src, dst, first):
        every = all_of(n_space, src, dst, sems.at[first], sems.at[first + 1])
        every.wait_recv()
        return every

    book_copies = around(lambda k: code_ref, lambda k: book_ref.at[x], 0)

    def fill_a(d):
        msg_a[d] = blocks_a[send_ref[d]]

    def fill_b(d):
        msg_b[d] = blocks_b[send_ref[d]]

    to_space(n_space, fill_a, msg_a, recv_a, sems.at[0], sems.at[1])
    to_space(n_space, fill_b, msg_b, recv_b, sems.at[2], sems.at[3])
    recv_a[me] = blocks_a[send_ref[me]]
    recv_b[me] = blocks_b[send_ref[me]]

    row_i = lax.broadcasted_iota(jnp.int32, (WIDTH, WIDTH), 0)
    col_i = lax.broadcasted_iota(jnp.int32, (WIDTH, WIDTH), 1)
    tri_ref[...] = jnp.where(row_i < col_i, 1.0, 0.0).astype(BF16)
    tris_ref[...] = jnp.where(row_i > col_i, 1.0, 0.0).astype(BF16)
    for j, row in enumerate(harmonic_rows(rays_ref[0:1, :], rays_ref[1:2, :], rays_ref[2:3, :])):
        harm_ref[j : j + 1, :] = row
    words_ref[...] = jnp.zeros_like(words_ref)
    u = lax.broadcasted_iota(jnp.int32, (SIDE, WIDTH), 0).astype(F32) - (SIDE - 1) * 0.5

    def message(t):
        return jnp.concatenate([recv_a[tile_ref[t, l]] for l in range(LIST)], axis=1).astype(F32)

    def v_rows(t, v):
        return pl.ds(pl.multiple_of(t * TILE_PIX + v * SIDE, SIDE), SIDE)

    def absorb_step(t, carry):
        msg = message(t)
        cu, cv, ca, cb, cc, op = [msg[i : i + 1] for i in range(GEO)]
        high, low = msg[6:7], msg[7:8]
        du = u - cu
        base_u = (-0.5 * LOG2E) * ca * du * du
        cross = (-LOG2E) * cb * du
        curve = (-0.5 * LOG2E) * cc
        for v in range(SIDE):
            rows = slice(v * SIDE, (v + 1) * SIDE)
            dv = (v - (SIDE - 1) * 0.5) - cv
            e = jnp.exp2(base_u + cross * dv + curve * dv * dv)
            lg = jnp.log2(1.0 - op * e)
            lg_hi = lg.astype(BF16)
            e_ref[v_rows(t, v), :] = e
            log_ref[rows, :] = lg_hi
            log_ref[TILE_PIX + v * SIDE : TILE_PIX + (v + 1) * SIDE, :] = (
                lg - lg_hi.astype(F32)
            ).astype(BF16)
        cum_ref[:, :half] = nn(log_ref[:, :half], tri_ref[:half, :half])
        cum_ref[:, half:] = nn(log_ref[...], tri_ref[:, half:])
        for v in range(SIDE):
            rows = slice(v * SIDE, (v + 1) * SIDE)
            cum = cum_ref[rows, :] + cum_ref[TILE_PIX + v * SIDE : TILE_PIX + (v + 1) * SIDE, :]
            wp = jnp.exp2(cum) * e_ref[v_rows(t, v), :]
            wp_ref[v_rows(t, v), :] = wp
            weight = wp * op
            weight_hi = weight.astype(BF16)
            wb_ref[v_rows(t, v), :] = weight_hi
            wl_ref[v_rows(t, v), :] = (weight - weight_hi.astype(F32)).astype(BF16)
        group = jnp.floor(high * 0.25)
        part = high - 4.0 * group
        word_row = lax.broadcasted_iota(jnp.int32, (256, 1), 0).astype(F32)
        for c in range(4):
            key = jnp.where(part == float(c), low, -1.0)
            hot_ref[t, c * 256 : (c + 1) * 256, :] = jnp.where(word_row == key, 1.0, 0.0).astype(
                BF16
            )
        looked_all = nn(book_ref[...].reshape(n_code * COEF, GWORDS), hot_ref[t])
        looked = jnp.where(group == 0.0, looked_all[:COEF], 0.0)
        for g in range(1, GROUPS):
            looked = jnp.where(group == float(g), looked_all[g * COEF : (g + 1) * COEF], looked)
        look_ref[t] = looked.astype(BF16)
        return carry

    for copy in book_copies:
        copy.wait()
    every_a = finish(msg_a, recv_a, 0)
    lax.fori_loop(0, tiles, absorb_step, 0)

    def unpair(ref, d):
        pairs = ref[d].astype(F32)
        rows = [pairs[:, i * BLOCK : (i + 1) * BLOCK] for i in range(PAIRS_B)]
        return jnp.concatenate(rows + [jnp.zeros((16 - RESID, BLOCK), F32)], axis=0)

    def color_step(t, carry):
        pix = lanes_of(t, TILE_PIX)
        resid = jnp.concatenate([unpair(recv_b, tile_ref[t, l]) for l in range(LIST)], axis=1)
        looked = look_ref[t].astype(F32)
        eight = lax.broadcasted_iota(jnp.int32, (8, WIDTH), 0)
        palette = jnp.concatenate(
            [looked[:16] + resid, looked[16:], jnp.where(eight == 0, 0.5, 0.0)], axis=0
        ).astype(BF16)
        palette = nn(perm_ref[...], palette).astype(BF16)
        weight = wb_ref[pix, :]
        weight_lo = wl_ref[pix, :]
        mixed = nt(palette, weight) + nt(palette, weight_lo)
        harm = harm_ref[:, pix]
        image = jnp.concatenate(
            [
                jnp.sum(harm * mixed[ch * 16 : (ch + 1) * 16], axis=0, keepdims=True)
                + mixed[48:49]
                for ch in range(3)
            ],
            axis=0,
        )
        img_ref[:, pix] = image
        off = image - target_ref[:, pix].astype(F32) / 255.0
        total = off[0:1] + off[1:2] + off[2:3]
        pix8 = lax.broadcasted_iota(jnp.int32, (8, TILE_PIX), 0)
        grad = jnp.concatenate(
            [harm * off[ch : ch + 1] for ch in range(3)] + [jnp.where(pix8 == 0, total, 0.0)],
            axis=0,
        )
        grad_hi = grad.astype(BF16)
        grad_lo = (grad - grad_hi.astype(F32)).astype(BF16)
        g_ref[pix, :] = tn(grad_hi, palette) + tn(grad_lo, palette)
        color = nn(grad_hi, weight) + nn(grad_lo, weight) + nn(grad_hi, weight_lo)
        natural_ref[t] = tn(perm_ref[...], color.astype(BF16))[:COEF].astype(BF16)
        for j in range(4):
            for ch in range(3):
                row = color[ch * 16 + j : ch * 16 + j + 1]
                for l in range(LIST):
                    grads_ref[pl.ds((3 * j + ch) * slots + t * LIST + l, 1), :] = row[
                        :, l * BLOCK : (l + 1) * BLOCK
                    ]
        return carry

    every_b = finish(msg_b, recv_b, 2)
    lax.fori_loop(0, tiles, color_step, 0)

    slot_d = lax.broadcasted_iota(jnp.int32, (n_space, slots), 0)
    slot_hot = jnp.where(slot_d == tile_row_ref[...], 1.0, 0.0)
    slot_hot = jnp.concatenate([slot_hot, slot_hot], axis=1).astype(BF16)

    def to_slots(r, ref, row):
        part = grads_ref[r * slots : (r + 1) * slots, :]
        part_hi = part.astype(BF16).astype(F32)
        both = jnp.concatenate([part_hi, part - part_hi], axis=0).astype(BF16)
        put_rows(ref, row, nn(slot_hot, both))

    for r in range(RESID):
        to_slots(r, stage_ref, r)

    def fill_r(d):
        for i in range(PAIRS_B):
            msg_r[d, :, i * BLOCK : (i + 1) * BLOCK] = stage_ref[
                pl.ds(pl.multiple_of(d * STAGE, STAGE) + 2 * i, 2), :
            ].astype(BF16)

    to_space(n_space, fill_r, msg_r, recv_r, sems.at[4], sems.at[5])
    fill_r(me)
    recv_r[me] = msg_r[me]

    def word_step(t, carry):
        group = jnp.floor(message(t)[6:7] * 0.25)
        natural = natural_ref[t].astype(F32)
        masked = jnp.concatenate(
            [jnp.where(group == float(g), natural, 0.0).astype(BF16) for g in range(GROUPS)], axis=0
        )
        words_ref[...] += nt(masked, hot_ref[t])
        return carry

    lax.fori_loop(0, tiles, word_step, 0)
    for g in range(GROUPS):
        mine_ref[g] = words_ref[g * COEF : (g + 1) * COEF, :].astype(BF16)
    word_copies = around(
        lambda k: mine_ref.at[lax.rem(x + k, n_code)], lambda k: theirs_ref.at[k - 1], 3
    )

    def foot_step(t, carry):
        msg = message(t)
        cu, cv, ca, cb, cc, op = [msg[i : i + 1] for i in range(GEO)]
        du = u - cu
        for v in range(SIDE):
            rows = slice(v * SIDE, (v + 1) * SIDE)
            wg_ref[rows, :] = (wp_ref[v_rows(t, v), :] * g_ref[v_rows(t, v), :] * op).astype(BF16)
        cum_ref[:TILE_PIX, half:] = nn(wg_ref[:, half:], tris_ref[half:, half:])
        cum_ref[:TILE_PIX, :half] = nn(wg_ref[...], tris_ref[:, :half])
        s_zero = jnp.zeros((SIDE, WIDTH), F32)
        s_one = jnp.zeros((SIDE, WIDTH), F32)
        s_two = jnp.zeros((SIDE, WIDTH), F32)
        for v in range(SIDE):
            rows = slice(v * SIDE, (v + 1) * SIDE)
            e = e_ref[v_rows(t, v), :]
            p = wp_ref[v_rows(t, v), :] * g_ref[v_rows(t, v), :] - cum_ref[rows, :] * (
                e / (1.0 - op * e)
            )
            dv = (v - (SIDE - 1) * 0.5) - cv
            pd = p * dv
            s_zero = s_zero + p
            s_one = s_one + pd
            s_two = s_two + pd * dv
        m_zero = jnp.sum(s_zero, axis=0, keepdims=True)
        m_u = jnp.sum(s_zero * du, axis=0, keepdims=True)
        m_uu = jnp.sum(s_zero * du * du, axis=0, keepdims=True)
        m_v = jnp.sum(s_one, axis=0, keepdims=True)
        m_uv = jnp.sum(s_one * du, axis=0, keepdims=True)
        m_vv = jnp.sum(s_two, axis=0, keepdims=True)
        rows_back = [
            op * (ca * m_u + cb * m_v),
            op * (cb * m_u + cc * m_v),
            -0.5 * op * m_uu,
            -op * m_uv,
            -0.5 * op * m_vv,
            m_zero,
        ]
        for r, row in enumerate(rows_back):
            for l in range(LIST):
                grads_ref[pl.ds((RESID + r) * slots + t * LIST + l, 1), :] = row[
                    :, l * BLOCK : (l + 1) * BLOCK
                ]
        return carry

    lax.fori_loop(0, tiles, foot_step, 0)
    for r in range(GEO):
        to_slots(RESID + r, stage_t_ref, 4 + r)
    for copy in word_copies:
        copy.wait()
    total = words_ref[pl.ds(pl.multiple_of(x * COEF, COEF), COEF), :]
    for k in range(n_code - 1):
        total = total + theirs_ref[k].astype(F32)
    wide_ref[...] = nn(spread_ref[...], total.astype(BF16))
    row8 = lax.broadcasted_iota(jnp.int32, (8, BLOCK), 0)

    def fill_t(d):
        own = pl.ds(pl.multiple_of(d * STAGE, STAGE), 8)
        word = wide_ref[pl.ds(pl.multiple_of(d // 8 * 8, 8), 8), lanes_of(lax.rem(d, 8))]
        stage_t_ref[own, :] = jnp.where(row8 < 4, word, stage_t_ref[own, :])
        for i in range(PAIRS_T):
            msg_t[d, :, i * BLOCK : (i + 1) * BLOCK] = stage_t_ref[
                pl.ds(pl.multiple_of(d * STAGE, STAGE) + 2 * i, 2), :
            ].astype(BF16)

    to_space(n_space, fill_t, msg_t, recv_t, sems.at[6], sems.at[7])
    fill_t(me)
    recv_t[me] = msg_t[me]

    own_b = lax.broadcasted_iota(jnp.int32, (blocks + 8, n_space), 0)
    own_hot = jnp.where(own_b == send_row_ref[...], 1.0, 0.0)
    own_hot = jnp.where(own_b == blocks, 1.0, own_hot).astype(BF16)

    def spread_pairs(ref, stage, pairs):
        def one(d, carry):
            for i in range(pairs):
                stage[pl.ds(pl.multiple_of(d * STAGE, STAGE) + 2 * i, 2), :] = ref[
                    d, :, i * BLOCK : (i + 1) * BLOCK
                ].astype(F32)
            return carry

        lax.fori_loop(0, n_space, one, 0, unroll=4)

    def owned(stage, row):
        return nn(own_hot, get_rows(stage, row, n_space).astype(BF16))

    every_r = finish(msg_r, recv_r, 4)
    spread_pairs(recv_r, stage_ref, PAIRS_B)
    for r in range(RESID):
        put_rows(own_ref, r, owned(stage_ref, r)[:blocks])

    def write_resid(b, carry):
        own_resid_ref[:, lanes_of(b)] = own_ref[pl.ds(pl.multiple_of(b * STAGE, STAGE), STAGE), :][
            :RESID
        ]
        return carry

    lax.fori_loop(0, blocks, write_resid, 0, unroll=4)
    width = part_ref.shape[2]
    resid_copies = around(
        lambda k: own_resid_ref.at[:, lanes_of(lax.rem(x + k, n_code), width)],
        lambda k: part_ref.at[k - 1],
        6,
    )
    for copy in resid_copies:
        copy.wait()
    total = own_resid_ref[:, lanes_of(x, width)]
    for k in range(n_code - 1):
        total = total + part_ref[k]
    resid_out_ref[:, lanes_of(x, width)] = total
    resid_copies = around(
        lambda k: resid_out_ref.at[:, lanes_of(x, width)],
        lambda k: resid_out_ref.at[:, lanes_of(x, width)],
        9,
    )

    every_t = finish(msg_t, recv_t, 6)
    spread_pairs(recv_t, stage_t_ref, PAIRS_T)
    line_ref[...] = jnp.concatenate(
        [owned(stage_t_ref, r)[blocks : blocks + 1] for r in range(3)], axis=1
    )
    plane, place = me // 8, lax.rem(me, 8)
    lines_ref[plane, place] = line_ref[...]
    near = []
    for k in range(1, 8):
        near.append(
            pltpu.make_async_remote_copy(
                src_ref=line_ref,
                dst_ref=lines_ref.at[plane, place],
                send_sem=near_send.at[k - 1],
                recv_sem=near_recv.at[k - 1],
                device_id={"space": plane * 8 + lax.rem(place + k, 8)},
                device_id_type=MESH,
            )
        )
        near[-1].start()
    for copy in near:
        copy.wait()
    planes = n_space // 8
    far = []
    for k in range(1, planes):
        far.append(
            pltpu.make_async_remote_copy(
                src_ref=lines_ref.at[plane],
                dst_ref=lines_ref.at[plane],
                send_sem=far_send.at[k - 1],
                recv_sem=far_recv.at[k - 1],
                device_id={"space": lax.rem(plane + k, planes) * 8 + place},
                device_id_type=MESH,
            )
        )
        far[-1].start()
    for r in range(GEO):
        put_rows(own_ref, r, owned(stage_t_ref, 4 + r)[:blocks])

    def write_foot(b, carry):
        foot_ref[:, lanes_of(b)] = own_ref[pl.ds(pl.multiple_of(b * STAGE, STAGE), 8), :][:GEO]
        return carry

    lax.fori_loop(0, blocks, write_foot, 0, unroll=4)
    for copy in far:
        copy.wait()
    for d in range(n_space):
        for i in range(3):
            row = d // 8 * 3 + i
            code_out_ref[row : row + 1, d % 8 * BLOCK : (d % 8 + 1) * BLOCK] = lines_ref[
                d // 8, d % 8, :, i * BLOCK : (i + 1) * BLOCK
            ]
    for copy in resid_copies:
        copy.wait()
    for every in (every_a, every_b, every_r, every_t):
        every.wait_send()


def on_device(geometry, codebook, word_ids, residual, send_list, tile_list, rays, target):
    blocks = word_ids.shape[0] // BLOCK
    n_space = lax.axis_size("space")
    n_code = lax.axis_size("code")
    perm, spread = constants()
    tiles = tile_list.shape[1]
    pixels = rays.shape[2]
    splats = blocks * BLOCK
    sent = send_list[0, 0]
    vm = pltpu.VMEM
    dma = pltpu.SemaphoreType.DMA
    image, foot, resid_grad, code_grad = pl.pallas_call(
        functools.partial(step_kernel, n_space, n_code),
        out_shape=(
            jax.ShapeDtypeStruct((3, pixels), F32),
            jax.ShapeDtypeStruct((GEO, splats), F32),
            jax.ShapeDtypeStruct((RESID, splats), F32),
            jax.ShapeDtypeStruct((COEF, GWORDS), F32),
        ),
        in_specs=[pl.BlockSpec(memory_space=pltpu.SMEM)] * 2 + [pl.BlockSpec(memory_space=vm)] * 10,
        out_specs=(pl.BlockSpec(memory_space=vm),) * 4,
        scratch_shapes=[
            vm((blocks, 8, BLOCK), BF16),
            vm((blocks, 2, PAIRS_B * BLOCK), BF16),
            vm((n_space, 8, BLOCK), BF16),
            vm((n_space, 2, PAIRS_B * BLOCK), BF16),
            vm((n_space, 8, BLOCK), BF16),
            vm((n_space, 2, PAIRS_B * BLOCK), BF16),
            vm((n_code, COEF, GWORDS), BF16),
            vm((pixels, WIDTH), F32),
            vm((pixels, WIDTH), F32),
            vm((pixels, WIDTH), BF16),
            vm((pixels, WIDTH), BF16),
            vm((pixels, WIDTH), F32),
            vm((tiles, GWORDS, WIDTH), BF16),
            vm((tiles, COEF, WIDTH), BF16),
            vm((tiles, COEF, WIDTH), BF16),
            vm((2 * TILE_PIX, WIDTH), BF16),
            vm((2 * TILE_PIX, WIDTH), F32),
            vm((TILE_PIX, WIDTH), BF16),
            vm((WIDTH, WIDTH), BF16),
            vm((WIDTH, WIDTH), BF16),
            vm((16, pixels), F32),
            vm((GROUPS * COEF, GWORDS), F32),
            vm((n_code, COEF, GWORDS), BF16),
            vm((n_code - 1, COEF, GWORDS), BF16),
            vm((n_space, GWORDS), F32),
            vm(((RESID + GEO) * tiles * LIST, BLOCK), F32),
            vm((n_space * STAGE, BLOCK), F32),
            vm((n_space * STAGE, BLOCK), F32),
            vm((n_space, 2, PAIRS_B * BLOCK), BF16),
            vm((n_space, 2, PAIRS_B * BLOCK), BF16),
            vm((n_space, 2, PAIRS_T * BLOCK), BF16),
            vm((n_space, 2, PAIRS_T * BLOCK), BF16),
            vm((blocks * STAGE, BLOCK), F32),
            vm((RESID, splats), F32),
            vm((n_code - 1, RESID, splats // n_code), F32),
            vm((1, 3 * BLOCK), F32),
            vm((n_space // 8, 8, 1, 3 * BLOCK), F32),
            dma((8,)),
            dma((4 * (n_code - 1),)),
            dma((4 * (n_code - 1),)),
            dma((7,)),
            dma((7,)),
            dma((n_space // 8 - 1,)),
            dma((n_space // 8 - 1,)),
        ],
        compiler_params=pltpu.CompilerParams(
            collective_id=0, has_side_effects=True, vmem_limit_bytes=56 * 2**20
        ),
        name="step",
    )(
        sent,
        tile_list[0],
        sent.reshape(1, n_space),
        tile_list.reshape(1, tiles * LIST),
        geometry[0],
        word_ids.reshape(blocks, BLOCK),
        residual,
        codebook,
        rays[0],
        target[0],
        perm,
        spread,
    )
    return (image[None], foot[None], resid_grad, code_grad)


def solution(mesh):
    placed = (
        P("code", None, "space"),
        P(None, "code"),
        P("space"),
        P(None, "space"),
        P("code", "space", None),
        P("code", "space", None),
        P("code", None, "space"),
        P("code", None, "space"),
    )
    return jax.shard_map(
        on_device,
        mesh=mesh,
        in_specs=placed,
        out_specs=(
            P("code", None, "space"),
            P("code", None, "space"),
            P(None, "space"),
            P(None, "code"),
        ),
        check_vma=False,
    )
```

```python
import functools

import jax
import jax.numpy as jnp
import numpy as np
from jax import lax
from jax.experimental import pallas as pl
from jax.experimental.pallas import tpu as pltpu
from jax.sharding import PartitionSpec as P

WORDS = 4096
COEF = 48
RESID = 12
GEO = 6
BLOCK = 128
LIST = 4
SIDE = 16
TILE_PIX = 256
WIDTH = LIST * BLOCK
GROUPS = 4
GWORDS = WORDS // GROUPS
PAIRS_B = RESID // 2
PAIRS_T = GEO // 2
STAGE = 16
LOG2E = 1.4426950408889634
F32 = jnp.float32
BF16 = jnp.bfloat16
MESH = pl.DeviceIdType.MESH

band_zero = 0.28209479177387814
band_one = 0.4886025119029199
band_two = (
    1.0925484305920792,
    -1.0925484305920792,
    0.31539156525252005,
    -1.0925484305920792,
    0.5462742152960396,
)
band_three = (
    -0.5900435899266435,
    2.890611442640554,
    -0.4570457994644658,
    0.3731763325901154,
    -0.4570457994644658,
    1.445305721320277,
    -0.5900435899266435,
)


def harmonic_rows(ray_x, ray_y, ray_z):
    length = jnp.sqrt(ray_x * ray_x + ray_y * ray_y + ray_z * ray_z)
    x = ray_x / length
    y = ray_y / length
    z = ray_z / length
    xx, yy, zz = x * x, y * y, z * z
    return [
        band_zero * jnp.ones_like(x),
        -band_one * y,
        band_one * z,
        -band_one * x,
        band_two[0] * x * y,
        band_two[1] * y * z,
        band_two[2] * (2.0 * zz - xx - yy),
        band_two[3] * x * z,
        band_two[4] * (xx - yy),
        band_three[0] * y * (3.0 * xx - yy),
        band_three[1] * x * y * z,
        band_three[2] * y * (4.0 * zz - xx - yy),
        band_three[3] * z * (2.0 * zz - 3.0 * xx - 3.0 * yy),
        band_three[4] * x * (4.0 * zz - xx - yy),
        band_three[5] * z * (xx - yy),
        band_three[6] * x * (xx - 3.0 * yy),
    ]


def nn(a, b):
    return lax.dot_general(a, b, (((1,), (0,)), ((), ())), preferred_element_type=F32)


def nt(a, b):
    return lax.dot_general(a, b, (((1,), (1,)), ((), ())), preferred_element_type=F32)


def tn(a, b):
    return lax.dot_general(a, b, (((0,), (0,)), ((), ())), preferred_element_type=F32)


def greet(n_space, n_code):
    me, x = lax.axis_index("space"), lax.axis_index("code")
    barrier = pltpu.get_barrier_semaphore()

    def hello(k, carry):
        for d in (lax.rem(me + k, n_space), lax.rem(me + n_space - k, n_space)):
            pl.semaphore_signal(barrier, inc=1, device_id={"space": d}, device_id_type=MESH)
        return carry

    lax.fori_loop(1, n_space // 2, hello, 0, unroll=3)
    pl.semaphore_signal(
        barrier,
        inc=1,
        device_id={"space": lax.rem(me + n_space // 2, n_space)},
        device_id_type=MESH,
    )
    for k in range(1, n_code):
        pl.semaphore_signal(
            barrier, inc=1, device_id={"code": lax.rem(x + k, n_code)}, device_id_type=MESH
        )
    return barrier


def to_space(n_space, fill, src, dst, send_sem, recv_sem):
    me = lax.axis_index("space")

    def one(d):
        if fill is not None:
            fill(d)
        pltpu.make_async_remote_copy(
            src_ref=src.at[d],
            dst_ref=dst.at[me],
            send_sem=send_sem,
            recv_sem=recv_sem,
            device_id={"space": d},
            device_id_type=MESH,
        ).start()

    def pair(k, carry):
        one(lax.rem(me + k, n_space))
        one(lax.rem(me + n_space - k, n_space))
        return carry

    lax.fori_loop(1, n_space // 2, pair, 0, unroll=3)
    one(lax.rem(me + n_space // 2, n_space))


def all_of(n_space, src, dst, send_sem, recv_sem):
    me = lax.axis_index("space")
    return pltpu.make_async_remote_copy(
        src_ref=src.at[pl.ds(0, n_space - 1)],
        dst_ref=dst.at[pl.ds(0, n_space - 1)],
        send_sem=send_sem,
        recv_sem=recv_sem,
        device_id={"space": lax.rem(me + 1, n_space)},
        device_id_type=MESH,
    )


def constants():
    perm = np.zeros((56, 56), np.float32)
    for j in range(16):
        for ch in range(3):
            perm[ch * 16 + j, 3 * j + ch] = 1.0
    perm[48, 48] = 1.0
    spread = np.zeros((128, COEF), np.float32)
    for k in range(COEF):
        spread[k // 3 * 8 + k % 3, k] = 1.0
    return jnp.asarray(perm, BF16), jnp.asarray(spread, BF16)


def put_rows(ref, row, value):
    ref[pl.ds(row, value.shape[0], stride=STAGE), :] = value


def get_rows(ref, row, count):
    return ref[pl.ds(row, count, stride=STAGE), :]


def step_kernel(
    n_space,
    n_code,
    send_ref,
    tile_ref,
    send_row_ref,
    geo_ref,
    word_ref,
    resid_ref,
    code_ref,
    rays_ref,
    target_ref,
    perm_ref,
    spread_ref,
    img_ref,
    foot_ref,
    resid_out_ref,
    code_out_ref,
    blocks_a,
    blocks_b,
    msg_a,
    msg_b,
    recv_a,
    recv_b,
    book_ref,
    e_ref,
    wp_ref,
    wb_ref,
    wl_ref,
    g_ref,
    hot_ref,
    look_ref,
    natural_ref,
    log_ref,
    cum_ref,
    wg_ref,
    tri_ref,
    tris_ref,
    harm_ref,
    words_ref,
    mine_ref,
    theirs_ref,
    wide_ref,
    grads_ref,
    stage_ref,
    stage_t_ref,
    msg_r,
    recv_r,
    msg_t,
    recv_t,
    own_ref,
    own_resid_ref,
    part_ref,
    lines_out,
    lines_in,
    near_ref,
    code_lines,
    sems,
    code_send,
    code_recv,
    near_send,
    near_recv,
    far_send,
    far_recv,
):
    me, x = lax.axis_index("space"), lax.axis_index("code")
    tiles = tile_ref.shape[1]
    slots = tiles * LIST
    blocks = blocks_a.shape[0]
    half = WIDTH // 2
    barrier = greet(n_space, n_code)

    def lanes_of(i, width=BLOCK):
        return pl.ds(pl.multiple_of(i * width, width), width)

    def build(b, carry):
        ids = word_ref[pl.ds(b, 1), :]
        high = (ids >> 8).astype(F32)
        low = (ids & 255).astype(F32)
        geo = geo_ref[:, lanes_of(b)].astype(F32)
        blocks_a[b] = jnp.concatenate([geo, high, low], axis=0).astype(BF16)
        return carry

    lax.fori_loop(0, blocks, build, 0, unroll=4)
    book_ref[x] = code_ref[...]
    pl.semaphore_wait(barrier, n_space + n_code - 2)

    def around(src, dst, first):
        copies = []
        for k in range(1, n_code):
            copies.append(
                pltpu.make_async_remote_copy(
                    src_ref=src(k),
                    dst_ref=dst(k),
                    send_sem=code_send.at[first + k - 1],
                    recv_sem=code_recv.at[first + k - 1],
                    device_id={"code": lax.rem(x + k, n_code)},
                    device_id_type=MESH,
                )
            )
            copies[-1].start()
        return copies

    def finish(src, dst, first):
        every = all_of(n_space, src, dst, sems.at[first], sems.at[first + 1])
        every.wait_recv()
        return every

    book_copies = around(lambda k: code_ref, lambda k: book_ref.at[x], 0)

    def fill_a(d):
        msg_a[d] = blocks_a[send_ref[d]]

    def fill_b(d):
        msg_b[d] = blocks_b[send_ref[d]]

    to_space(n_space, fill_a, msg_a, recv_a, sems.at[0], sems.at[1])
    def build_b(b, carry):
        resid = resid_ref[:, lanes_of(b)].astype(F32)
        blocks_b[b] = jnp.concatenate(
            [resid[2 * i : 2 * i + 2] for i in range(PAIRS_B)], axis=1
        ).astype(BF16)
        return carry

    lax.fori_loop(0, blocks, build_b, 0, unroll=4)
    to_space(n_space, fill_b, msg_b, recv_b, sems.at[2], sems.at[3])
    recv_a[me] = blocks_a[send_ref[me]]
    recv_b[me] = blocks_b[send_ref[me]]

    row_i = lax.broadcasted_iota(jnp.int32, (WIDTH, WIDTH), 0)
    col_i = lax.broadcasted_iota(jnp.int32, (WIDTH, WIDTH), 1)
    tri_ref[...] = jnp.where(row_i < col_i, 1.0, 0.0).astype(BF16)
    tris_ref[...] = jnp.where(row_i > col_i, 1.0, 0.0).astype(BF16)
    for j, row in enumerate(harmonic_rows(rays_ref[0], rays_ref[1], rays_ref[2])):
        harm_ref[j : j + 1, :] = row
    words_ref[...] = jnp.zeros_like(words_ref)
    u = lax.broadcasted_iota(jnp.int32, (SIDE, WIDTH), 0).astype(F32) - (SIDE - 1) * 0.5

    def message(t):
        return jnp.concatenate([recv_a[tile_ref[l, t]] for l in range(LIST)], axis=1).astype(F32)

    def v_rows(t, v):
        return pl.ds(pl.multiple_of(t * TILE_PIX + v * SIDE, SIDE), SIDE)

    def absorb_step(t, carry):
        msg = message(t)
        cu, cv, ca, cb, cc, op = [msg[i : i + 1] for i in range(GEO)]
        high, low = msg[6:7], msg[7:8]
        du = u - cu
        base_u = (-0.5 * LOG2E) * ca * du * du
        cross = (-LOG2E) * cb * du
        curve = (-0.5 * LOG2E) * cc
        for v in range(SIDE):
            rows = slice(v * SIDE, (v + 1) * SIDE)
            dv = (v - (SIDE - 1) * 0.5) - cv
            e = jnp.exp2(base_u + cross * dv + curve * dv * dv)
            lg = jnp.log2(1.0 - op * e)
            lg_hi = lg.astype(BF16)
            e_ref[v_rows(t, v), :] = e
            log_ref[rows, :] = lg_hi
            log_ref[TILE_PIX + v * SIDE : TILE_PIX + (v + 1) * SIDE, :] = (
                lg - lg_hi.astype(F32)
            ).astype(BF16)
        cum_ref[:, :half] = nn(log_ref[:, :half], tri_ref[:half, :half])
        cum_ref[:, half:] = nn(log_ref[...], tri_ref[:, half:])
        for v in range(SIDE):
            rows = slice(v * SIDE, (v + 1) * SIDE)
            cum = cum_ref[rows, :] + cum_ref[TILE_PIX + v * SIDE : TILE_PIX + (v + 1) * SIDE, :]
            wp = jnp.exp2(cum) * e_ref[v_rows(t, v), :]
            wp_ref[v_rows(t, v), :] = wp
            weight = wp * op
            weight_hi = weight.astype(BF16)
            wb_ref[v_rows(t, v), :] = weight_hi
            wl_ref[v_rows(t, v), :] = (weight - weight_hi.astype(F32)).astype(BF16)
        group = jnp.floor(high * 0.25)
        part = high - 4.0 * group
        word_row = lax.broadcasted_iota(jnp.int32, (256, 1), 0).astype(F32)
        for c in range(4):
            key = jnp.where(part == float(c), low, -1.0)
            hot_ref[t, c * 256 : (c + 1) * 256, :] = jnp.where(word_row == key, 1.0, 0.0).astype(
                BF16
            )
        looked_all = nn(book_ref[...].reshape(n_code * COEF, GWORDS), hot_ref[t])
        looked = jnp.where(group == 0.0, looked_all[:COEF], 0.0)
        for g in range(1, GROUPS):
            looked = jnp.where(group == float(g), looked_all[g * COEF : (g + 1) * COEF], looked)
        look_ref[t] = looked.astype(BF16)
        return carry

    for copy in book_copies:
        copy.wait()
    every_a = finish(msg_a, recv_a, 0)
    lax.fori_loop(0, tiles, absorb_step, 0)

    def unpair(ref, d):
        pairs = ref[d].astype(F32)
        rows = [pairs[:, i * BLOCK : (i + 1) * BLOCK] for i in range(PAIRS_B)]
        return jnp.concatenate(rows + [jnp.zeros((16 - RESID, BLOCK), F32)], axis=0)

    def color_step(t, carry):
        pix = lanes_of(t, TILE_PIX)
        resid = jnp.concatenate([unpair(recv_b, tile_ref[l, t]) for l in range(LIST)], axis=1)
        looked = look_ref[t].astype(F32)
        eight = lax.broadcasted_iota(jnp.int32, (8, WIDTH), 0)
        palette = jnp.concatenate(
            [looked[:16] + resid, looked[16:], jnp.where(eight == 0, 0.5, 0.0)], axis=0
        ).astype(BF16)
        palette = nn(perm_ref[...], palette).astype(BF16)
        weight = wb_ref[pix, :]
        weight_lo = wl_ref[pix, :]
        mixed = nt(palette, weight) + nt(palette, weight_lo)
        harm = harm_ref[:, pix]
        image = [
            jnp.sum(harm * mixed[ch * 16 : (ch + 1) * 16], axis=0, keepdims=True) + mixed[48:49]
            for ch in range(3)
        ]
        for ch in range(3):
            img_ref[ch, :, pix] = image[ch]
        off = [image[ch] - target_ref[ch, :, pix].astype(F32) / 255.0 for ch in range(3)]
        total = off[0] + off[1] + off[2]
        pix8 = lax.broadcasted_iota(jnp.int32, (8, TILE_PIX), 0)
        grad = jnp.concatenate(
            [harm * off[ch] for ch in range(3)] + [jnp.where(pix8 == 0, total, 0.0)],
            axis=0,
        )
        grad_hi = grad.astype(BF16)
        grad_lo = (grad - grad_hi.astype(F32)).astype(BF16)
        both = jnp.concatenate([grad_hi, grad_lo], axis=0)
        g_ref[pix, :] = tn(both, jnp.concatenate([palette, palette], axis=0))
        color = nn(both, weight)
        color = color[:56] + color[56:] + nn(grad_hi, weight_lo)
        natural_ref[t] = tn(perm_ref[...], color.astype(BF16))[:COEF].astype(BF16)
        for j in range(4):
            for ch in range(3):
                row = color[ch * 16 + j : ch * 16 + j + 1]
                for l in range(LIST):
                    grads_ref[pl.ds((3 * j + ch) * slots + l * tiles + t, 1), :] = row[
                        :, l * BLOCK : (l + 1) * BLOCK
                    ]
        return carry

    every_b = finish(msg_b, recv_b, 2)
    lax.fori_loop(0, tiles, color_step, 0, unroll=2)

    lane_d = lax.broadcasted_iota(jnp.int32, (1, n_space), 1)
    slot_hot = [
        jnp.where(lane_d == tile_ref[l, t], 1.0, 0.0) for l in range(LIST) for t in range(tiles)
    ]
    slot_hot = jnp.concatenate(slot_hot * 2, axis=0).astype(BF16)

    def to_slots(r, ref, row):
        part = grads_ref[r * slots : (r + 1) * slots, :]
        part_hi = part.astype(BF16).astype(F32)
        both = jnp.concatenate([part_hi, part - part_hi], axis=0).astype(BF16)
        put_rows(ref, row, tn(slot_hot, both))

    for r in range(RESID):
        to_slots(r, stage_ref, r)

    def fill_r(d):
        for i in range(PAIRS_B):
            msg_r[d, :, i * BLOCK : (i + 1) * BLOCK] = stage_ref[
                pl.ds(pl.multiple_of(d * STAGE, STAGE) + 2 * i, 2), :
            ].astype(BF16)

    to_space(n_space, fill_r, msg_r, recv_r, sems.at[4], sems.at[5])
    fill_r(me)
    recv_r[me] = msg_r[me]

    def word_step(t, carry):
        group = jnp.floor(message(t)[6:7] * 0.25)
        natural = natural_ref[t].astype(F32)
        masked = jnp.concatenate(
            [jnp.where(group == float(g), natural, 0.0).astype(BF16) for g in range(GROUPS)], axis=0
        )
        words_ref[...] += nt(masked, hot_ref[t])
        return carry

    lax.fori_loop(0, tiles, word_step, 0)
    for g in range(GROUPS):
        mine_ref[g] = words_ref[g * COEF : (g + 1) * COEF, :].astype(BF16)
    word_copies = around(
        lambda k: mine_ref.at[lax.rem(x + k, n_code)], lambda k: theirs_ref.at[k - 1], 3
    )

    def foot_step(t, carry):
        msg = message(t)
        cu, cv, ca, cb, cc, op = [msg[i : i + 1] for i in range(GEO)]
        du = u - cu
        for v in range(SIDE):
            rows = slice(v * SIDE, (v + 1) * SIDE)
            wg_ref[rows, :] = (wp_ref[v_rows(t, v), :] * g_ref[v_rows(t, v), :] * op).astype(BF16)
        cum_ref[:TILE_PIX, half:] = nn(wg_ref[:, half:], tris_ref[half:, half:])
        cum_ref[:TILE_PIX, :half] = nn(wg_ref[...], tris_ref[:, :half])
        s_zero = jnp.zeros((SIDE, WIDTH), F32)
        s_one = jnp.zeros((SIDE, WIDTH), F32)
        s_two = jnp.zeros((SIDE, WIDTH), F32)
        for v in range(SIDE):
            rows = slice(v * SIDE, (v + 1) * SIDE)
            e = e_ref[v_rows(t, v), :]
            p = wp_ref[v_rows(t, v), :] * g_ref[v_rows(t, v), :] - cum_ref[rows, :] * (
                e / (1.0 - op * e)
            )
            dv = (v - (SIDE - 1) * 0.5) - cv
            pd = p * dv
            s_zero = s_zero + p
            s_one = s_one + pd
            s_two = s_two + pd * dv
        m_zero = jnp.sum(s_zero, axis=0, keepdims=True)
        m_u = jnp.sum(s_zero * du, axis=0, keepdims=True)
        m_uu = jnp.sum(s_zero * du * du, axis=0, keepdims=True)
        m_v = jnp.sum(s_one, axis=0, keepdims=True)
        m_uv = jnp.sum(s_one * du, axis=0, keepdims=True)
        m_vv = jnp.sum(s_two, axis=0, keepdims=True)
        rows_back = [
            op * (ca * m_u + cb * m_v),
            op * (cb * m_u + cc * m_v),
            -0.5 * op * m_uu,
            -op * m_uv,
            -0.5 * op * m_vv,
            m_zero,
        ]
        for r, row in enumerate(rows_back):
            for l in range(LIST):
                grads_ref[pl.ds((RESID + r) * slots + l * tiles + t, 1), :] = row[
                    :, l * BLOCK : (l + 1) * BLOCK
                ]
        return carry

    lax.fori_loop(0, tiles, foot_step, 0)
    for copy in word_copies:
        copy.wait()
    total = words_ref[pl.ds(pl.multiple_of(x * COEF, COEF), COEF), :]
    for k in range(n_code - 1):
        total = total + theirs_ref[k].astype(F32)
    wide_ref[...] = nn(spread_ref[...], total.astype(BF16))
    planes, crowd = n_space // 8, 8
    plane, place = me // crowd, lax.rem(me, crowd)
    for j in range(planes):
        third = wide_ref[8 * j + 2 : 8 * j + 3, :]
        third = jnp.concatenate([third[:, : GWORDS // 2], third[:, GWORDS // 2 :]], axis=0)
        lines_out[j] = jnp.concatenate([wide_ref[8 * j : 8 * j + 2, :], third], axis=1).astype(BF16)

    def along(src, dst, first):
        copies = []
        for k in range(1, planes):
            there = lax.rem(plane + k, planes)
            copies.append(
                pltpu.make_async_remote_copy(
                    src_ref=src(there),
                    dst_ref=dst,
                    send_sem=far_send.at[first + k - 1],
                    recv_sem=far_recv.at[first + k - 1],
                    device_id={"space": there * crowd + place},
                    device_id_type=MESH,
                )
            )
            copies[-1].start()
        return copies

    line_copies = along(lambda there: lines_out.at[there], lines_in.at[plane], 0)
    lines_in[plane] = lines_out[plane]
    for r in range(GEO):
        to_slots(RESID + r, stage_t_ref, r)

    def fill_t(d):
        for i in range(PAIRS_T):
            msg_t[d, :, i * BLOCK : (i + 1) * BLOCK] = stage_t_ref[
                pl.ds(pl.multiple_of(d * STAGE, STAGE) + 2 * i, 2), :
            ].astype(BF16)

    to_space(n_space, fill_t, msg_t, recv_t, sems.at[6], sems.at[7])
    fill_t(me)
    recv_t[me] = msg_t[me]

    for copy in line_copies:
        copy.wait()
    total = lines_in[0].astype(F32)
    for j in range(1, planes):
        total = total + lines_in[j].astype(F32)
    near_ref[place] = total
    near = []
    for k in range(1, crowd):
        near.append(
            pltpu.make_async_remote_copy(
                src_ref=near_ref.at[place],
                dst_ref=near_ref.at[place],
                send_sem=near_send.at[k - 1],
                recv_sem=near_recv.at[k - 1],
                device_id={"space": plane * crowd + lax.rem(place + k, crowd)},
                device_id_type=MESH,
            )
        )
        near[-1].start()

    own_b = lax.broadcasted_iota(jnp.int32, (blocks, n_space), 0)
    own_hot = jnp.where(own_b == send_row_ref[...], 1.0, 0.0).astype(BF16)

    def spread_pairs(ref, stage, pairs):
        def one(d, carry):
            for i in range(pairs):
                stage[pl.ds(pl.multiple_of(d * STAGE, STAGE) + 2 * i, 2), :] = ref[
                    d, :, i * BLOCK : (i + 1) * BLOCK
                ].astype(F32)
            return carry

        lax.fori_loop(0, n_space, one, 0, unroll=4)

    def owned(stage, row):
        return nn(own_hot, get_rows(stage, row, n_space).astype(BF16))

    every_r = finish(msg_r, recv_r, 4)
    spread_pairs(recv_r, stage_ref, PAIRS_B)
    for r in range(RESID):
        put_rows(own_ref, r, owned(stage_ref, r))

    def write_resid(b, carry):
        own_resid_ref[:, lanes_of(b)] = own_ref[pl.ds(pl.multiple_of(b * STAGE, STAGE), STAGE), :][
            :RESID
        ]
        return carry

    lax.fori_loop(0, blocks, write_resid, 0, unroll=4)
    width = part_ref.shape[2]
    resid_copies = around(
        lambda k: own_resid_ref.at[:, lanes_of(lax.rem(x + k, n_code), width)],
        lambda k: part_ref.at[k - 1],
        6,
    )
    for copy in near:
        copy.wait()
    total = near_ref[0]
    for k in range(1, crowd):
        total = total + near_ref[k]
    code_lines[plane] = total.astype(BF16)
    far = along(lambda there: code_lines.at[plane], code_lines.at[plane], planes - 1)
    for copy in resid_copies:
        copy.wait()
    total = own_resid_ref[:, lanes_of(x, width)]
    for k in range(n_code - 1):
        total = total + part_ref[k]
    resid_out_ref[:, lanes_of(x, width)] = total
    resid_copies = around(
        lambda k: resid_out_ref.at[:, lanes_of(x, width)],
        lambda k: resid_out_ref.at[:, lanes_of(x, width)],
        9,
    )

    every_t = finish(msg_t, recv_t, 6)
    spread_pairs(recv_t, stage_t_ref, PAIRS_T)
    for r in range(GEO):
        foot_ref[r] = owned(stage_t_ref, r)
    for copy in far:
        copy.wait()
    for j in range(planes):
        rows = code_lines[j].astype(F32)
        code_out_ref[3 * j : 3 * j + 2, :] = rows[:, :GWORDS]
        code_out_ref[3 * j + 2 : 3 * j + 3, : GWORDS // 2] = rows[0:1, GWORDS:]
        code_out_ref[3 * j + 2 : 3 * j + 3, GWORDS // 2 :] = rows[1:2, GWORDS:]
    for copy in resid_copies:
        copy.wait()
    for every in (every_a, every_b, every_r, every_t):
        every.wait_send()


def on_device(geometry, codebook, word_ids, residual, send_list, tile_list, rays, target):
    blocks = word_ids.shape[0] // BLOCK
    n_space = lax.axis_size("space")
    n_code = lax.axis_size("code")
    perm, spread = constants()
    tiles = tile_list.shape[1]
    pixels = rays.shape[2]
    splats = blocks * BLOCK
    sent = send_list[0, 0]
    vm = pltpu.VMEM
    dma = pltpu.SemaphoreType.DMA
    image, foot, resid_grad, code_grad = pl.pallas_call(
        functools.partial(step_kernel, n_space, n_code),
        out_shape=(
            jax.ShapeDtypeStruct((3, 1, pixels), F32),
            jax.ShapeDtypeStruct((GEO, blocks, BLOCK), F32),
            jax.ShapeDtypeStruct((RESID, splats), F32),
            jax.ShapeDtypeStruct((COEF, GWORDS), F32),
        ),
        in_specs=[pl.BlockSpec(memory_space=pltpu.SMEM)] * 2 + [pl.BlockSpec(memory_space=vm)] * 9,
        out_specs=(pl.BlockSpec(memory_space=vm),) * 4,
        scratch_shapes=[
            vm((blocks, 8, BLOCK), BF16),
            vm((blocks, 2, PAIRS_B * BLOCK), BF16),
            vm((n_space, 8, BLOCK), BF16),
            vm((n_space, 2, PAIRS_B * BLOCK), BF16),
            vm((n_space, 8, BLOCK), BF16),
            vm((n_space, 2, PAIRS_B * BLOCK), BF16),
            vm((n_code, COEF, GWORDS), BF16),
            vm((pixels, WIDTH), F32),
            vm((pixels, WIDTH), F32),
            vm((pixels, WIDTH), BF16),
            vm((pixels, WIDTH), BF16),
            vm((pixels, WIDTH), F32),
            vm((tiles, GWORDS, WIDTH), BF16),
            vm((tiles, COEF, WIDTH), BF16),
            vm((tiles, COEF, WIDTH), BF16),
            vm((2 * TILE_PIX, WIDTH), BF16),
            vm((2 * TILE_PIX, WIDTH), F32),
            vm((TILE_PIX, WIDTH), BF16),
            vm((WIDTH, WIDTH), BF16),
            vm((WIDTH, WIDTH), BF16),
            vm((16, pixels), F32),
            vm((GROUPS * COEF, GWORDS), F32),
            vm((n_code, COEF, GWORDS), BF16),
            vm((n_code - 1, COEF, GWORDS), BF16),
            vm((n_space, GWORDS), F32),
            vm(((RESID + GEO) * tiles * LIST, BLOCK), F32),
            vm((n_space * STAGE, BLOCK), F32),
            vm((n_space * STAGE, BLOCK), F32),
            vm((n_space, 2, PAIRS_B * BLOCK), BF16),
            vm((n_space, 2, PAIRS_B * BLOCK), BF16),
            vm((n_space, 2, PAIRS_T * BLOCK), BF16),
            vm((n_space, 2, PAIRS_T * BLOCK), BF16),
            vm((blocks * STAGE, BLOCK), F32),
            vm((RESID, splats), F32),
            vm((n_code - 1, RESID, splats // n_code), F32),
            vm((n_space // 8, 2, 3 * GWORDS // 2), BF16),
            vm((n_space // 8, 2, 3 * GWORDS // 2), BF16),
            vm((8, 2, 3 * GWORDS // 2), F32),
            vm((n_space // 8, 2, 3 * GWORDS // 2), BF16),
            dma((8,)),
            dma((4 * (n_code - 1),)),
            dma((4 * (n_code - 1),)),
            dma((7,)),
            dma((7,)),
            dma((2 * (n_space // 8 - 1),)),
            dma((2 * (n_space // 8 - 1),)),
        ],
        compiler_params=pltpu.CompilerParams(
            collective_id=0, has_side_effects=True, vmem_limit_bytes=56 * 2**20
        ),
        name="step",
    )(
        sent,
        tile_list[0].T,
        sent.reshape(1, n_space),
        geometry[0],
        word_ids.reshape(blocks, BLOCK),
        residual,
        codebook,
        jnp.swapaxes(rays, 0, 1),
        jnp.swapaxes(target, 0, 1),
        perm,
        spread,
    )
    image = jnp.swapaxes(image, 0, 1)
    foot = jnp.swapaxes(foot.reshape(GEO, 1, splats), 0, 1)
    return (image, foot, resid_grad, code_grad)


def solution(mesh):
    placed = (
        P("code", None, "space"),
        P(None, "code"),
        P("space"),
        P(None, "space"),
        P("code", "space", None),
        P("code", "space", None),
        P("code", None, "space"),
        P("code", None, "space"),
    )
    return jax.shard_map(
        on_device,
        mesh=mesh,
        in_specs=placed,
        out_specs=(
            P("code", None, "space"),
            P("code", None, "space"),
            P(None, "space"),
            P(None, "code"),
        ),
        check_vma=False,
    )
```

```python
import functools

import jax
import jax.numpy as jnp
import numpy as np
from jax import lax
from jax.experimental import pallas as pl
from jax.experimental.pallas import tpu as pltpu
from jax.sharding import PartitionSpec as P

WORDS = 4096
COEF = 48
RESID = 12
GEO = 6
BLOCK = 128
LIST = 4
SIDE = 16
TILE_PIX = 256
WIDTH = LIST * BLOCK
GROUPS = 4
GWORDS = WORDS // GROUPS
PAIRS_B = RESID // 2
PAIRS_T = GEO // 2
STAGE = 16
LOG2E = 1.4426950408889634
F32 = jnp.float32
BF16 = jnp.bfloat16
MESH = pl.DeviceIdType.MESH

band_zero = 0.28209479177387814
band_one = 0.4886025119029199
band_two = (
    1.0925484305920792,
    -1.0925484305920792,
    0.31539156525252005,
    -1.0925484305920792,
    0.5462742152960396,
)
band_three = (
    -0.5900435899266435,
    2.890611442640554,
    -0.4570457994644658,
    0.3731763325901154,
    -0.4570457994644658,
    1.445305721320277,
    -0.5900435899266435,
)


def harmonic_rows(ray_x, ray_y, ray_z):
    length = jnp.sqrt(ray_x * ray_x + ray_y * ray_y + ray_z * ray_z)
    x = ray_x / length
    y = ray_y / length
    z = ray_z / length
    xx, yy, zz = x * x, y * y, z * z
    return [
        band_zero * jnp.ones_like(x),
        -band_one * y,
        band_one * z,
        -band_one * x,
        band_two[0] * x * y,
        band_two[1] * y * z,
        band_two[2] * (2.0 * zz - xx - yy),
        band_two[3] * x * z,
        band_two[4] * (xx - yy),
        band_three[0] * y * (3.0 * xx - yy),
        band_three[1] * x * y * z,
        band_three[2] * y * (4.0 * zz - xx - yy),
        band_three[3] * z * (2.0 * zz - 3.0 * xx - 3.0 * yy),
        band_three[4] * x * (4.0 * zz - xx - yy),
        band_three[5] * z * (xx - yy),
        band_three[6] * x * (xx - 3.0 * yy),
    ]


def nn(a, b):
    return lax.dot_general(a, b, (((1,), (0,)), ((), ())), preferred_element_type=F32)


def nt(a, b):
    return lax.dot_general(a, b, (((1,), (1,)), ((), ())), preferred_element_type=F32)


def tn(a, b):
    return lax.dot_general(a, b, (((0,), (0,)), ((), ())), preferred_element_type=F32)


def greet(n_space, n_code):
    me, x = lax.axis_index("space"), lax.axis_index("code")
    barrier = pltpu.get_barrier_semaphore()

    def hello(k, carry):
        for d in (lax.rem(me + k, n_space), lax.rem(me + n_space - k, n_space)):
            pl.semaphore_signal(barrier, inc=1, device_id={"space": d}, device_id_type=MESH)
        return carry

    lax.fori_loop(1, n_space // 2, hello, 0, unroll=3)
    pl.semaphore_signal(
        barrier,
        inc=1,
        device_id={"space": lax.rem(me + n_space // 2, n_space)},
        device_id_type=MESH,
    )
    for k in range(1, n_code):
        pl.semaphore_signal(
            barrier, inc=1, device_id={"code": lax.rem(x + k, n_code)}, device_id_type=MESH
        )
    return barrier


def to_space(n_space, fill, src, dst, send_sem, recv_sem, first=1, stop=None):
    me = lax.axis_index("space")

    def one(d):
        if fill is not None:
            fill(d)
        pltpu.make_async_remote_copy(
            src_ref=src.at[d],
            dst_ref=dst.at[me],
            send_sem=send_sem,
            recv_sem=recv_sem,
            device_id={"space": d},
            device_id_type=MESH,
        ).start()

    def pair(k, carry):
        one(lax.rem(me + k, n_space))
        one(lax.rem(me + n_space - k, n_space))
        return carry

    lax.fori_loop(first, stop or n_space // 2, pair, 0, unroll=3)
    if stop is None:
        one(lax.rem(me + n_space // 2, n_space))


def all_of(n_space, src, dst, send_sem, recv_sem):
    me = lax.axis_index("space")
    return pltpu.make_async_remote_copy(
        src_ref=src.at[pl.ds(0, n_space - 1)],
        dst_ref=dst.at[pl.ds(0, n_space - 1)],
        send_sem=send_sem,
        recv_sem=recv_sem,
        device_id={"space": lax.rem(me + 1, n_space)},
        device_id_type=MESH,
    )


def constants():
    perm = np.zeros((56, 56), np.float32)
    for j in range(16):
        for ch in range(3):
            perm[ch * 16 + j, 3 * j + ch] = 1.0
    perm[48, 48] = 1.0
    spread = np.zeros((128, COEF), np.float32)
    for k in range(COEF):
        spread[k // 3 * 8 + k % 3, k] = 1.0
    return jnp.asarray(perm, BF16), jnp.asarray(spread, BF16)


def put_rows(ref, row, value):
    ref[pl.ds(row, value.shape[0], stride=STAGE), :] = value


def get_rows(ref, row, count):
    return ref[pl.ds(row, count, stride=STAGE), :]


def step_kernel(
    n_space,
    n_code,
    send_ref,
    tile_ref,
    send_row_ref,
    geo_ref,
    word_ref,
    resid_ref,
    code_ref,
    rays_ref,
    target_ref,
    perm_ref,
    spread_ref,
    img_ref,
    foot_ref,
    resid_out_ref,
    code_out_ref,
    blocks_a,
    blocks_b,
    msg_a,
    msg_b,
    recv_a,
    recv_b,
    book_ref,
    e_ref,
    wp_ref,
    wb_ref,
    wl_ref,
    g_ref,
    hot_ref,
    look_ref,
    natural_ref,
    log_ref,
    cum_ref,
    wg_ref,
    tri_ref,
    tris_ref,
    spot_ref,
    harm_ref,
    words_ref,
    mine_ref,
    theirs_ref,
    wide_ref,
    grads_ref,
    stage_ref,
    stage_t_ref,
    msg_r,
    recv_r,
    msg_t,
    recv_t,
    own_resid_ref,
    part_ref,
    sum_ref,
    lines_out,
    lines_in,
    near_ref,
    code_lines,
    sems,
    code_send,
    code_recv,
    near_send,
    near_recv,
    far_send,
    far_recv,
):
    me, x = lax.axis_index("space"), lax.axis_index("code")
    tiles = tile_ref.shape[1]
    slots = tiles * LIST
    blocks = blocks_a.shape[0]
    half = WIDTH // 2
    barrier = greet(n_space, n_code)

    def lanes_of(i, width=BLOCK):
        return pl.ds(pl.multiple_of(i * width, width), width)

    def build(b, carry):
        ids = word_ref[pl.ds(b, 1), :]
        high = (ids >> 8).astype(F32)
        low = (ids & 255).astype(F32)
        geo = geo_ref[:, lanes_of(b)].astype(F32)
        blocks_a[b] = jnp.concatenate([geo, high, low], axis=0).astype(BF16)
        return carry

    lax.fori_loop(0, blocks, build, 0, unroll=4)
    book_ref[x] = code_ref[...]
    pl.semaphore_wait(barrier, n_space + n_code - 2)

    def around(src, dst, first):
        copies = []
        for k in range(1, n_code):
            copies.append(
                pltpu.make_async_remote_copy(
                    src_ref=src(k),
                    dst_ref=dst(k),
                    send_sem=code_send.at[first + k - 1],
                    recv_sem=code_recv.at[first + k - 1],
                    device_id={"code": lax.rem(x + k, n_code)},
                    device_id_type=MESH,
                )
            )
            copies[-1].start()
        return copies

    def finish(src, dst, first):
        every = all_of(n_space, src, dst, sems.at[first], sems.at[first + 1])
        every.wait_recv()
        return every

    book_copies = around(lambda k: code_ref, lambda k: book_ref.at[x], 0)

    def fill_a(d):
        msg_a[d] = blocks_a[send_ref[d]]

    def fill_b(d):
        msg_b[d] = blocks_b[send_ref[d]]

    to_space(n_space, fill_a, msg_a, recv_a, sems.at[0], sems.at[1])
    def build_b(b, carry):
        resid = resid_ref[:, lanes_of(b)].astype(F32)
        blocks_b[b] = jnp.concatenate(
            [resid[2 * i : 2 * i + 2] for i in range(PAIRS_B)], axis=1
        ).astype(BF16)
        return carry

    lax.fori_loop(0, blocks, build_b, 0, unroll=4)
    to_space(n_space, fill_b, msg_b, recv_b, sems.at[2], sems.at[3])
    recv_a[me] = blocks_a[send_ref[me]]
    recv_b[me] = blocks_b[send_ref[me]]

    row_i = lax.broadcasted_iota(jnp.int32, (WIDTH, WIDTH), 0)
    col_i = lax.broadcasted_iota(jnp.int32, (WIDTH, WIDTH), 1)
    tri_ref[...] = jnp.where(row_i < col_i, 1.0, 0.0).astype(BF16)
    tris_ref[...] = jnp.where(row_i > col_i, 1.0, 0.0).astype(BF16)
    for j, row in enumerate(harmonic_rows(rays_ref[0], rays_ref[1], rays_ref[2])):
        harm_ref[j : j + 1, :] = row
    words_ref[...] = jnp.zeros_like(words_ref)
    u = lax.broadcasted_iota(jnp.int32, (SIDE, WIDTH), 0).astype(F32) - (SIDE - 1) * 0.5

    def message(t):
        return jnp.concatenate([recv_a[tile_ref[l, t]] for l in range(LIST)], axis=1).astype(F32)

    def v_rows(t, v):
        return pl.ds(pl.multiple_of(t * TILE_PIX + v * SIDE, SIDE), SIDE)

    def absorb_step(t, carry):
        msg = message(t)
        cu, cv, ca, cb, cc, op = [msg[i : i + 1] for i in range(GEO)]
        high, low = msg[6:7], msg[7:8]
        du = u - cu
        base_u = (-0.5 * LOG2E) * ca * du * du
        cross = (-LOG2E) * cb * du
        curve = (-0.5 * LOG2E) * cc
        for v in range(SIDE):
            rows = slice(v * SIDE, (v + 1) * SIDE)
            dv = (v - (SIDE - 1) * 0.5) - cv
            e = jnp.exp2(base_u + cross * dv + curve * dv * dv)
            lg = jnp.log2(1.0 - op * e)
            lg_hi = lg.astype(BF16)
            e_ref[v_rows(t, v), :] = e
            log_ref[rows, :] = lg_hi
            log_ref[TILE_PIX + v * SIDE : TILE_PIX + (v + 1) * SIDE, :] = (
                lg - lg_hi.astype(F32)
            ).astype(BF16)
        cum_ref[:, :half] = nn(log_ref[:, :half], tri_ref[:half, :half])
        cum_ref[:, half:] = nn(log_ref[...], tri_ref[:, half:])
        for v in range(SIDE):
            rows = slice(v * SIDE, (v + 1) * SIDE)
            cum = cum_ref[rows, :] + cum_ref[TILE_PIX + v * SIDE : TILE_PIX + (v + 1) * SIDE, :]
            wp = jnp.exp2(cum) * e_ref[v_rows(t, v), :]
            wp_ref[v_rows(t, v), :] = wp
            weight = wp * op
            weight_hi = weight.astype(BF16)
            wb_ref[v_rows(t, v), :] = weight_hi
            wl_ref[v_rows(t, v), :] = (weight - weight_hi.astype(F32)).astype(BF16)
        group = jnp.floor(high * 0.25)
        part = high - 4.0 * group
        word_row = lax.broadcasted_iota(jnp.int32, (256, 1), 0).astype(F32)
        for c in range(4):
            key = jnp.where(part == float(c), low, -1.0)
            hot_ref[t, c * 256 : (c + 1) * 256, :] = jnp.where(word_row == key, 1.0, 0.0).astype(
                BF16
            )
        looked_all = nn(book_ref[...].reshape(n_code * COEF, GWORDS), hot_ref[t])
        looked = jnp.where(group == 0.0, looked_all[:COEF], 0.0)
        for g in range(1, GROUPS):
            looked = jnp.where(group == float(g), looked_all[g * COEF : (g + 1) * COEF], looked)
        look_ref[t] = looked.astype(BF16)
        return carry

    for copy in book_copies:
        copy.wait()
    every_a = finish(msg_a, recv_a, 0)
    lax.fori_loop(0, tiles, absorb_step, 0)

    def unpair(ref, d):
        pairs = ref[d].astype(F32)
        rows = [pairs[:, i * BLOCK : (i + 1) * BLOCK] for i in range(PAIRS_B)]
        return jnp.concatenate(rows + [jnp.zeros((16 - RESID, BLOCK), F32)], axis=0)

    def color_step(t, carry):
        pix = lanes_of(t, TILE_PIX)
        resid = jnp.concatenate([unpair(recv_b, tile_ref[l, t]) for l in range(LIST)], axis=1)
        looked = look_ref[t].astype(F32)
        eight = lax.broadcasted_iota(jnp.int32, (8, WIDTH), 0)
        palette = jnp.concatenate(
            [looked[:16] + resid, looked[16:], jnp.where(eight == 0, 0.5, 0.0)], axis=0
        ).astype(BF16)
        palette = nn(perm_ref[...], palette).astype(BF16)
        weight = wb_ref[pix, :]
        weight_lo = wl_ref[pix, :]
        mixed = nt(palette, weight) + nt(palette, weight_lo)
        harm = harm_ref[:, pix]
        image = [
            jnp.sum(harm * mixed[ch * 16 : (ch + 1) * 16], axis=0, keepdims=True) + mixed[48:49]
            for ch in range(3)
        ]
        for ch in range(3):
            img_ref[ch, :, pix] = image[ch]
        off = [image[ch] - target_ref[ch, :, pix].astype(F32) / 255.0 for ch in range(3)]
        total = off[0] + off[1] + off[2]
        pix8 = lax.broadcasted_iota(jnp.int32, (8, TILE_PIX), 0)
        grad = jnp.concatenate(
            [harm * off[ch] for ch in range(3)] + [jnp.where(pix8 == 0, total, 0.0)],
            axis=0,
        )
        grad_hi = grad.astype(BF16)
        grad_lo = (grad - grad_hi.astype(F32)).astype(BF16)
        both = jnp.concatenate([grad_hi, grad_lo], axis=0)
        g_ref[pix, :] = tn(both, jnp.concatenate([palette, palette], axis=0))
        color = nn(both, weight)
        color = color[:56] + color[56:] + nn(grad_hi, weight_lo)
        natural_ref[t] = tn(perm_ref[...], color.astype(BF16))[:COEF].astype(BF16)
        for j in range(4):
            for ch in range(3):
                row = color[ch * 16 + j : ch * 16 + j + 1]
                for l in range(LIST):
                    grads_ref[pl.ds((3 * j + ch) * slots + l * tiles + t, 1), :] = row[
                        :, l * BLOCK : (l + 1) * BLOCK
                    ]
        return carry

    lane_d = lax.broadcasted_iota(jnp.int32, (1, n_space), 1)
    slot_hot = [
        jnp.where(lane_d == tile_ref[l, t], 1.0, 0.0) for l in range(LIST) for t in range(tiles)
    ]
    spot_ref[...] = jnp.concatenate(slot_hot * (n_space // slots), axis=0).T.astype(BF16)
    every_b = finish(msg_b, recv_b, 2)
    lax.fori_loop(0, tiles, color_step, 0, unroll=4)

    def to_slots(r, ref, row):
        part = grads_ref[r * slots : (r + 1) * slots, :]
        part_hi = part.astype(BF16).astype(F32)
        both = jnp.concatenate([part_hi, part - part_hi], axis=0).astype(BF16)
        put_rows(ref, row, nn(spot_ref[:, : 2 * slots], both))

    for r in range(RESID):
        to_slots(r, stage_ref, r)

    def fill_r(d):
        for i in range(PAIRS_B):
            msg_r[d, :, i * BLOCK : (i + 1) * BLOCK] = stage_ref[
                pl.ds(pl.multiple_of(d * STAGE, STAGE) + 2 * i, 2), :
            ].astype(BF16)

    to_space(n_space, fill_r, msg_r, recv_r, sems.at[4], sems.at[5])
    fill_r(me)
    recv_r[me] = msg_r[me]

    def word_step(t, carry):
        group = jnp.floor(message(t)[6:7] * 0.25)
        natural = natural_ref[t].astype(F32)
        masked = jnp.concatenate(
            [jnp.where(group == float(g), natural, 0.0).astype(BF16) for g in range(GROUPS)], axis=0
        )
        words_ref[...] += nt(masked, hot_ref[t])
        return carry

    lax.fori_loop(0, tiles, word_step, 0)
    for g in range(GROUPS):
        mine_ref[g] = words_ref[g * COEF : (g + 1) * COEF, :].astype(BF16)
    word_copies = around(
        lambda k: mine_ref.at[lax.rem(x + k, n_code)], lambda k: theirs_ref.at[k - 1], 3
    )

    def foot_step(t, carry):
        msg = message(t)
        cu, cv, ca, cb, cc, op = [msg[i : i + 1] for i in range(GEO)]
        du = u - cu
        for v in range(SIDE):
            rows = slice(v * SIDE, (v + 1) * SIDE)
            wg_ref[rows, :] = (wp_ref[v_rows(t, v), :] * g_ref[v_rows(t, v), :] * op).astype(BF16)
        cum_ref[:TILE_PIX, half:] = nn(wg_ref[:, half:], tris_ref[half:, half:])
        cum_ref[:TILE_PIX, :half] = nn(wg_ref[...], tris_ref[:, :half])
        s_zero = jnp.zeros((SIDE, WIDTH), F32)
        s_one = jnp.zeros((SIDE, WIDTH), F32)
        s_two = jnp.zeros((SIDE, WIDTH), F32)
        for v in range(SIDE):
            rows = slice(v * SIDE, (v + 1) * SIDE)
            e = e_ref[v_rows(t, v), :]
            p = wp_ref[v_rows(t, v), :] * g_ref[v_rows(t, v), :] - cum_ref[rows, :] * (
                e / (1.0 - op * e)
            )
            dv = (v - (SIDE - 1) * 0.5) - cv
            pd = p * dv
            s_zero = s_zero + p
            s_one = s_one + pd
            s_two = s_two + pd * dv
        m_zero = jnp.sum(s_zero, axis=0, keepdims=True)
        m_u = jnp.sum(s_zero * du, axis=0, keepdims=True)
        m_uu = jnp.sum(s_zero * du * du, axis=0, keepdims=True)
        m_v = jnp.sum(s_one, axis=0, keepdims=True)
        m_uv = jnp.sum(s_one * du, axis=0, keepdims=True)
        m_vv = jnp.sum(s_two, axis=0, keepdims=True)
        rows_back = [
            op * (ca * m_u + cb * m_v),
            op * (cb * m_u + cc * m_v),
            -0.5 * op * m_uu,
            -op * m_uv,
            -0.5 * op * m_vv,
            m_zero,
        ]
        for r, row in enumerate(rows_back):
            for l in range(LIST):
                grads_ref[pl.ds((RESID + r) * slots + l * tiles + t, 1), :] = row[
                    :, l * BLOCK : (l + 1) * BLOCK
                ]
        return carry

    lax.fori_loop(0, tiles, foot_step, 0)
    for copy in word_copies:
        copy.wait()
    total = words_ref[pl.ds(pl.multiple_of(x * COEF, COEF), COEF), :]
    for k in range(n_code - 1):
        total = total + theirs_ref[k].astype(F32)
    wide_ref[...] = nn(spread_ref[...], total.astype(BF16))
    planes, crowd = n_space // 8, 8
    plane, place = me // crowd, lax.rem(me, crowd)
    for j in range(planes):
        third = wide_ref[8 * j + 2 : 8 * j + 3, :]
        third = jnp.concatenate([third[:, : GWORDS // 2], third[:, GWORDS // 2 :]], axis=0)
        lines_out[j] = jnp.concatenate([wide_ref[8 * j : 8 * j + 2, :], third], axis=1).astype(BF16)

    def along(src, dst, first):
        copies = []
        for k in range(1, planes):
            there = lax.rem(plane + k, planes)
            copies.append(
                pltpu.make_async_remote_copy(
                    src_ref=src(there),
                    dst_ref=dst,
                    send_sem=far_send.at[first + k - 1],
                    recv_sem=far_recv.at[first + k - 1],
                    device_id={"space": there * crowd + place},
                    device_id_type=MESH,
                )
            )
            copies[-1].start()
        return copies

    line_copies = along(lambda there: lines_out.at[there], lines_in.at[plane], 0)
    lines_in[plane] = lines_out[plane]
    for r in range(GEO):
        to_slots(RESID + r, stage_t_ref, r)

    def fill_t(d):
        for i in range(PAIRS_T):
            msg_t[d, :, i * BLOCK : (i + 1) * BLOCK] = stage_t_ref[
                pl.ds(pl.multiple_of(d * STAGE, STAGE) + 2 * i, 2), :
            ].astype(BF16)

    own_b = lax.broadcasted_iota(jnp.int32, (blocks, n_space), 0)
    own_hot = jnp.where(own_b == send_row_ref[...], 1.0, 0.0).astype(BF16)

    def spread_pairs(ref, stage, pairs):
        def one(d, carry):
            for i in range(pairs):
                stage[pl.ds(pl.multiple_of(d * STAGE, STAGE) + 2 * i, 2), :] = ref[
                    d, :, i * BLOCK : (i + 1) * BLOCK
                ].astype(F32)
            return carry

        lax.fori_loop(0, n_space, one, 0, unroll=4)

    def owned(stage, row):
        return nn(own_hot, get_rows(stage, row, n_space).astype(BF16))

    every_r = finish(msg_r, recv_r, 4)
    spread_pairs(recv_r, stage_ref, PAIRS_B)
    share = blocks // n_code
    chunk = RESID * share

    def chunk_of(i):
        return pl.ds(pl.multiple_of(i * chunk, chunk), chunk)

    for r in range(RESID):
        own = owned(stage_ref, r)
        for c in range(n_code):
            at = c * chunk + r * share
            own_resid_ref[at : at + share, :] = own[c * share : (c + 1) * share]
    resid_copies = around(
        lambda k: own_resid_ref.at[chunk_of(lax.rem(x + k, n_code))],
        lambda k: part_ref.at[k - 1],
        6,
    )
    middle = n_space // 4 - 1
    to_space(n_space, fill_t, msg_t, recv_t, sems.at[6], sems.at[7], 1, middle)
    for copy in line_copies:
        copy.wait()
    total = lines_in[0].astype(F32)
    for j in range(1, planes):
        total = total + lines_in[j].astype(F32)
    near_ref[place] = total
    near = []
    for k in range(1, crowd):
        near.append(
            pltpu.make_async_remote_copy(
                src_ref=near_ref.at[place],
                dst_ref=near_ref.at[place],
                send_sem=near_send.at[k - 1],
                recv_sem=near_recv.at[k - 1],
                device_id={"space": plane * crowd + lax.rem(place + k, crowd)},
                device_id_type=MESH,
            )
        )
        near[-1].start()

    for copy in resid_copies:
        copy.wait()
    total = own_resid_ref[chunk_of(x), :]
    for k in range(n_code - 1):
        total = total + part_ref[k]
    sum_ref[chunk_of(x), :] = total
    resid_copies = around(
        lambda k: sum_ref.at[chunk_of(x)],
        lambda k: sum_ref.at[chunk_of(x)],
        9,
    )
    to_space(n_space, fill_t, msg_t, recv_t, sems.at[6], sems.at[7], middle)
    fill_t(me)
    recv_t[me] = msg_t[me]
    for copy in near:
        copy.wait()
    total = near_ref[0]
    for k in range(1, crowd):
        total = total + near_ref[k]
    code_lines[plane] = total.astype(BF16)
    far = along(lambda there: code_lines.at[plane], code_lines.at[plane], planes - 1)

    every_t = finish(msg_t, recv_t, 6)
    spread_pairs(recv_t, stage_t_ref, PAIRS_T)
    for r in range(GEO):
        foot_ref[r] = owned(stage_t_ref, r)
    for copy in far:
        copy.wait()
    for j in range(planes):
        rows = code_lines[j].astype(F32)
        code_out_ref[3 * j : 3 * j + 2, :] = rows[:, :GWORDS]
        code_out_ref[3 * j + 2 : 3 * j + 3, : GWORDS // 2] = rows[0:1, GWORDS:]
        code_out_ref[3 * j + 2 : 3 * j + 3, GWORDS // 2 :] = rows[1:2, GWORDS:]
    for copy in resid_copies:
        copy.wait()
    for b in range(blocks):
        at = b // share * chunk + b % share
        resid_out_ref[:, b * BLOCK : (b + 1) * BLOCK] = sum_ref[pl.ds(at, RESID, stride=share), :]
    for every in (every_a, every_b, every_r, every_t):
        every.wait_send()


def hand_over_kernel(*refs):
    sems = refs[-1]
    count = len(refs) // 2
    copies = [
        pltpu.make_async_copy(refs[i], refs[count + i], sems.at[i]) for i in range(count)
    ]
    for copy in copies:
        copy.start()
    for copy in copies:
        copy.wait()


def hand_over(arrays):
    return pl.pallas_call(
        hand_over_kernel,
        out_shape=tuple(jax.ShapeDtypeStruct(a.shape, a.dtype) for a in arrays),
        in_specs=[pl.BlockSpec(memory_space=pl.ANY)] * len(arrays),
        out_specs=(pl.BlockSpec(memory_space=pl.ANY),) * len(arrays),
        scratch_shapes=[pltpu.SemaphoreType.DMA((len(arrays),))],
        name="hand_over",
    )(*arrays)


def on_device(geometry, codebook, word_ids, residual, send_list, tile_list, rays, target):
    blocks = word_ids.shape[0] // BLOCK
    n_space = lax.axis_size("space")
    n_code = lax.axis_size("code")
    perm, spread = constants()
    tiles = tile_list.shape[1]
    pixels = rays.shape[2]
    splats = blocks * BLOCK
    sent = send_list[0, 0]
    vm = pltpu.VMEM
    dma = pltpu.SemaphoreType.DMA
    results = pl.pallas_call(
        functools.partial(step_kernel, n_space, n_code),
        out_shape=(
            jax.ShapeDtypeStruct((3, 1, pixels), F32),
            jax.ShapeDtypeStruct((GEO, blocks, BLOCK), F32),
            jax.ShapeDtypeStruct((RESID, splats), F32),
            jax.ShapeDtypeStruct((COEF, GWORDS), F32),
        ),
        in_specs=[pl.BlockSpec(memory_space=pltpu.SMEM)] * 2 + [pl.BlockSpec(memory_space=vm)] * 9,
        out_specs=(pl.BlockSpec(memory_space=vm),) * 4,
        scratch_shapes=[
            vm((blocks, 8, BLOCK), BF16),
            vm((blocks, 2, PAIRS_B * BLOCK), BF16),
            vm((n_space, 8, BLOCK), BF16),
            vm((n_space, 2, PAIRS_B * BLOCK), BF16),
            vm((n_space, 8, BLOCK), BF16),
            vm((n_space, 2, PAIRS_B * BLOCK), BF16),
            vm((n_code, COEF, GWORDS), BF16),
            vm((pixels, WIDTH), F32),
            vm((pixels, WIDTH), F32),
            vm((pixels, WIDTH), BF16),
            vm((pixels, WIDTH), BF16),
            vm((pixels, WIDTH), F32),
            vm((tiles, GWORDS, WIDTH), BF16),
            vm((tiles, COEF, WIDTH), BF16),
            vm((tiles, COEF, WIDTH), BF16),
            vm((2 * TILE_PIX, WIDTH), BF16),
            vm((2 * TILE_PIX, WIDTH), F32),
            vm((TILE_PIX, WIDTH), BF16),
            vm((WIDTH, WIDTH), BF16),
            vm((WIDTH, WIDTH), BF16),
            vm((n_space, n_space), BF16),
            vm((16, pixels), F32),
            vm((GROUPS * COEF, GWORDS), F32),
            vm((n_code, COEF, GWORDS), BF16),
            vm((n_code - 1, COEF, GWORDS), BF16),
            vm((n_space, GWORDS), F32),
            vm(((RESID + GEO) * tiles * LIST, BLOCK), F32),
            vm((n_space * STAGE, BLOCK), F32),
            vm((n_space * STAGE, BLOCK), F32),
            vm((n_space, 2, PAIRS_B * BLOCK), BF16),
            vm((n_space, 2, PAIRS_B * BLOCK), BF16),
            vm((n_space, 2, PAIRS_T * BLOCK), BF16),
            vm((n_space, 2, PAIRS_T * BLOCK), BF16),
            vm((RESID * blocks, BLOCK), F32),
            vm((n_code - 1, RESID * blocks // n_code, BLOCK), F32),
            vm((RESID * blocks, BLOCK), F32),
            vm((n_space // 8, 2, 3 * GWORDS // 2), BF16),
            vm((n_space // 8, 2, 3 * GWORDS // 2), BF16),
            vm((8, 2, 3 * GWORDS // 2), F32),
            vm((n_space // 8, 2, 3 * GWORDS // 2), BF16),
            dma((8,)),
            dma((4 * (n_code - 1),)),
            dma((4 * (n_code - 1),)),
            dma((7,)),
            dma((7,)),
            dma((2 * (n_space // 8 - 1),)),
            dma((2 * (n_space // 8 - 1),)),
        ],
        compiler_params=pltpu.CompilerParams(
            collective_id=0, has_side_effects=True, vmem_limit_bytes=56 * 2**20
        ),
        name="step",
    )(
        sent,
        tile_list[0].T,
        sent.reshape(1, n_space),
        geometry[0],
        word_ids.reshape(blocks, BLOCK),
        residual,
        codebook,
        jnp.swapaxes(rays, 0, 1),
        jnp.swapaxes(target, 0, 1),
        perm,
        spread,
    )
    image, foot, resid_grad, code_grad = hand_over(results)
    image = jnp.swapaxes(image, 0, 1)
    foot = jnp.swapaxes(foot.reshape(GEO, 1, splats), 0, 1)
    return (image, foot, resid_grad, code_grad)


def solution(mesh):
    placed = (
        P("code", None, "space"),
        P(None, "code"),
        P("space"),
        P(None, "space"),
        P("code", "space", None),
        P("code", "space", None),
        P("code", None, "space"),
        P("code", None, "space"),
    )
    return jax.shard_map(
        on_device,
        mesh=mesh,
        in_specs=placed,
        out_specs=(
            P("code", None, "space"),
            P("code", None, "space"),
            P(None, "space"),
            P(None, "code"),
        ),
        check_vma=False,
    )
```

```python
import functools

import jax
import jax.numpy as jnp
import numpy as np
from jax import lax
from jax.experimental import pallas as pl
from jax.experimental.pallas import tpu as pltpu
from jax.sharding import PartitionSpec as P

WORDS = 4096
COEF = 48
RESID = 12
GEO = 6
BLOCK = 128
LIST = 4
SIDE = 16
TILE_PIX = 256
WIDTH = LIST * BLOCK
GROUPS = 4
GWORDS = WORDS // GROUPS
PAIRS_B = RESID // 2
PAIRS_T = GEO // 2
STAGE = 16
LOG2E = 1.4426950408889634
F32 = jnp.float32
BF16 = jnp.bfloat16
MESH = pl.DeviceIdType.MESH

band_zero = 0.28209479177387814
band_one = 0.4886025119029199
band_two = (
    1.0925484305920792,
    -1.0925484305920792,
    0.31539156525252005,
    -1.0925484305920792,
    0.5462742152960396,
)
band_three = (
    -0.5900435899266435,
    2.890611442640554,
    -0.4570457994644658,
    0.3731763325901154,
    -0.4570457994644658,
    1.445305721320277,
    -0.5900435899266435,
)


def harmonic_rows(ray_x, ray_y, ray_z):
    length = jnp.sqrt(ray_x * ray_x + ray_y * ray_y + ray_z * ray_z)
    x = ray_x / length
    y = ray_y / length
    z = ray_z / length
    xx, yy, zz = x * x, y * y, z * z
    return [
        band_zero * jnp.ones_like(x),
        -band_one * y,
        band_one * z,
        -band_one * x,
        band_two[0] * x * y,
        band_two[1] * y * z,
        band_two[2] * (2.0 * zz - xx - yy),
        band_two[3] * x * z,
        band_two[4] * (xx - yy),
        band_three[0] * y * (3.0 * xx - yy),
        band_three[1] * x * y * z,
        band_three[2] * y * (4.0 * zz - xx - yy),
        band_three[3] * z * (2.0 * zz - 3.0 * xx - 3.0 * yy),
        band_three[4] * x * (4.0 * zz - xx - yy),
        band_three[5] * z * (xx - yy),
        band_three[6] * x * (xx - 3.0 * yy),
    ]


def nn(a, b):
    return lax.dot_general(a, b, (((1,), (0,)), ((), ())), preferred_element_type=F32)


def nt(a, b):
    return lax.dot_general(a, b, (((1,), (1,)), ((), ())), preferred_element_type=F32)


def tn(a, b):
    return lax.dot_general(a, b, (((0,), (0,)), ((), ())), preferred_element_type=F32)


def greet(n_space, n_code):
    me, x = lax.axis_index("space"), lax.axis_index("code")
    barrier = pltpu.get_barrier_semaphore()

    def hello(k, carry):
        for d in (lax.rem(me + k, n_space), lax.rem(me + n_space - k, n_space)):
            pl.semaphore_signal(barrier, inc=1, device_id={"space": d}, device_id_type=MESH)
        return carry

    lax.fori_loop(1, n_space // 2, hello, 0, unroll=3)
    pl.semaphore_signal(
        barrier,
        inc=1,
        device_id={"space": lax.rem(me + n_space // 2, n_space)},
        device_id_type=MESH,
    )
    for k in range(1, n_code):
        pl.semaphore_signal(
            barrier, inc=1, device_id={"code": lax.rem(x + k, n_code)}, device_id_type=MESH
        )
    return barrier


def to_space(n_space, fill, src, dst, send_sem, recv_sem, first=1, stop=None):
    me = lax.axis_index("space")

    def one(d):
        if fill is not None:
            fill(d)
        pltpu.make_async_remote_copy(
            src_ref=src.at[d],
            dst_ref=dst.at[me],
            send_sem=send_sem,
            recv_sem=recv_sem,
            device_id={"space": d},
            device_id_type=MESH,
        ).start()

    def pair(k, carry):
        one(lax.rem(me + k, n_space))
        one(lax.rem(me + n_space - k, n_space))
        return carry

    lax.fori_loop(first, stop or n_space // 2, pair, 0, unroll=3)
    if stop is None:
        one(lax.rem(me + n_space // 2, n_space))


def all_of(n_space, src, dst, send_sem, recv_sem):
    me = lax.axis_index("space")
    return pltpu.make_async_remote_copy(
        src_ref=src.at[pl.ds(0, n_space - 1)],
        dst_ref=dst.at[pl.ds(0, n_space - 1)],
        send_sem=send_sem,
        recv_sem=recv_sem,
        device_id={"space": lax.rem(me + 1, n_space)},
        device_id_type=MESH,
    )


def constants():
    perm = np.zeros((56, 56), np.float32)
    for j in range(16):
        for ch in range(3):
            perm[ch * 16 + j, 3 * j + ch] = 1.0
    perm[48, 48] = 1.0
    spread = np.zeros((128, COEF), np.float32)
    for k in range(COEF):
        spread[k // 3 * 8 + k % 3, k] = 1.0
    return jnp.asarray(perm, BF16), jnp.asarray(spread, BF16)


def put_rows(ref, row, value):
    ref[pl.ds(row, value.shape[0], stride=STAGE), :] = value


def get_rows(ref, row, count):
    return ref[pl.ds(row, count, stride=STAGE), :]


def step_kernel(
    n_space,
    n_code,
    send_ref,
    tile_ref,
    send_row_ref,
    geo_ref,
    word_ref,
    resid_ref,
    code_ref,
    rays_ref,
    target_ref,
    perm_ref,
    spread_ref,
    img_ref,
    foot_ref,
    resid_out_ref,
    code_out_ref,
    blocks_a,
    blocks_b,
    msg_a,
    msg_b,
    recv_a,
    recv_b,
    book_ref,
    e_ref,
    wp_ref,
    wb_ref,
    wl_ref,
    g_ref,
    hot_ref,
    look_ref,
    color_ref,
    both_ref,
    palette_ref,
    log_ref,
    cum_ref,
    wg_ref,
    tri_ref,
    tris_ref,
    spot_ref,
    harm_ref,
    words_ref,
    mine_ref,
    theirs_ref,
    wide_ref,
    grads_ref,
    stage_ref,
    stage_t_ref,
    msg_r,
    recv_r,
    msg_t,
    recv_t,
    own_resid_ref,
    part_ref,
    sum_ref,
    lines_out,
    lines_in,
    near_ref,
    code_lines,
    sems,
    code_send,
    code_recv,
    near_send,
    near_recv,
    far_send,
    far_recv,
):
    me, x = lax.axis_index("space"), lax.axis_index("code")
    tiles = tile_ref.shape[1]
    slots = tiles * LIST
    blocks = blocks_a.shape[0]
    half = WIDTH // 2
    barrier = greet(n_space, n_code)

    def lanes_of(i, width=BLOCK):
        return pl.ds(pl.multiple_of(i * width, width), width)

    def build(b, carry):
        ids = word_ref[pl.ds(b, 1), :]
        high = (ids >> 8).astype(F32)
        low = (ids & 255).astype(F32)
        geo = geo_ref[:, lanes_of(b)].astype(F32)
        blocks_a[b] = jnp.concatenate([geo, high, low], axis=0).astype(BF16)
        return carry

    lax.fori_loop(0, blocks, build, 0, unroll=4)
    book_ref[x] = code_ref[...]
    pl.semaphore_wait(barrier, n_space + n_code - 2)

    def around(src, dst, first):
        copies = []
        for k in range(1, n_code):
            copies.append(
                pltpu.make_async_remote_copy(
                    src_ref=src(k),
                    dst_ref=dst(k),
                    send_sem=code_send.at[first + k - 1],
                    recv_sem=code_recv.at[first + k - 1],
                    device_id={"code": lax.rem(x + k, n_code)},
                    device_id_type=MESH,
                )
            )
            copies[-1].start()
        return copies

    def finish(src, dst, first):
        every = all_of(n_space, src, dst, sems.at[first], sems.at[first + 1])
        every.wait_recv()
        return every

    book_copies = around(lambda k: code_ref, lambda k: book_ref.at[x], 0)

    def fill_a(d):
        msg_a[d] = blocks_a[send_ref[d]]

    def fill_b(d):
        msg_b[d] = blocks_b[send_ref[d]]

    to_space(n_space, fill_a, msg_a, recv_a, sems.at[0], sems.at[1])
    def build_b(b, carry):
        resid = resid_ref[:, lanes_of(b)].astype(F32)
        blocks_b[b] = jnp.concatenate(
            [resid[2 * i : 2 * i + 2] for i in range(PAIRS_B)], axis=1
        ).astype(BF16)
        return carry

    lax.fori_loop(0, blocks, build_b, 0, unroll=4)
    to_space(n_space, fill_b, msg_b, recv_b, sems.at[2], sems.at[3])
    recv_a[me] = blocks_a[send_ref[me]]
    recv_b[me] = blocks_b[send_ref[me]]

    row_i = lax.broadcasted_iota(jnp.int32, (WIDTH, WIDTH), 0)
    col_i = lax.broadcasted_iota(jnp.int32, (WIDTH, WIDTH), 1)
    tri_ref[...] = jnp.where(row_i < col_i, 1.0, 0.0).astype(BF16)
    tris_ref[...] = jnp.where(row_i > col_i, 1.0, 0.0).astype(BF16)
    for j, row in enumerate(harmonic_rows(rays_ref[0], rays_ref[1], rays_ref[2])):
        harm_ref[j : j + 1, :] = row
    words_ref[...] = jnp.zeros_like(words_ref)
    u = lax.broadcasted_iota(jnp.int32, (SIDE, WIDTH), 0).astype(F32) - (SIDE - 1) * 0.5

    def message(t):
        return jnp.concatenate([recv_a[tile_ref[l, t]] for l in range(LIST)], axis=1).astype(F32)

    def v_rows(t, v):
        return pl.ds(pl.multiple_of(t * TILE_PIX + v * SIDE, SIDE), SIDE)

    def absorb_step(t, carry):
        msg = message(t)
        cu, cv, ca, cb, cc, op = [msg[i : i + 1] for i in range(GEO)]
        high, low = msg[6:7], msg[7:8]
        du = u - cu
        base_u = (-0.5 * LOG2E) * ca * du * du
        cross = (-LOG2E) * cb * du
        curve = (-0.5 * LOG2E) * cc
        for v in range(SIDE):
            rows = slice(v * SIDE, (v + 1) * SIDE)
            dv = (v - (SIDE - 1) * 0.5) - cv
            e = jnp.exp2(base_u + cross * dv + curve * dv * dv)
            lg = jnp.log2(1.0 - op * e)
            lg_hi = lg.astype(BF16)
            e_ref[v_rows(t, v), :] = e
            log_ref[rows, :] = lg_hi
            log_ref[TILE_PIX + v * SIDE : TILE_PIX + (v + 1) * SIDE, :] = (
                lg - lg_hi.astype(F32)
            ).astype(BF16)
        cum_ref[:, :half] = nn(log_ref[:, :half], tri_ref[:half, :half])
        cum_ref[:, half:] = nn(log_ref[...], tri_ref[:, half:])
        for v in range(SIDE):
            rows = slice(v * SIDE, (v + 1) * SIDE)
            cum = cum_ref[rows, :] + cum_ref[TILE_PIX + v * SIDE : TILE_PIX + (v + 1) * SIDE, :]
            wp = jnp.exp2(cum) * e_ref[v_rows(t, v), :]
            wp_ref[v_rows(t, v), :] = wp
            weight = wp * op
            weight_hi = weight.astype(BF16)
            wb_ref[v_rows(t, v), :] = weight_hi
            wl_ref[v_rows(t, v), :] = (weight - weight_hi.astype(F32)).astype(BF16)
        group = jnp.floor(high * 0.25)
        part = high - 4.0 * group
        word_row = lax.broadcasted_iota(jnp.int32, (256, 1), 0).astype(F32)
        for c in range(4):
            key = jnp.where(part == float(c), low, -1.0)
            hot_ref[t, c * 256 : (c + 1) * 256, :] = jnp.where(word_row == key, 1.0, 0.0).astype(
                BF16
            )
        looked_all = nn(book_ref[...].reshape(n_code * COEF, GWORDS), hot_ref[t])
        looked = jnp.where(group == 0.0, looked_all[:COEF], 0.0)
        for g in range(1, GROUPS):
            looked = jnp.where(group == float(g), looked_all[g * COEF : (g + 1) * COEF], looked)
        look_ref[t] = looked.astype(BF16)
        return carry

    for copy in book_copies:
        copy.wait()
    every_a = finish(msg_a, recv_a, 0)
    lax.fori_loop(0, tiles, absorb_step, 0)

    def unpair(ref, d):
        pairs = ref[d].astype(F32)
        rows = [pairs[:, i * BLOCK : (i + 1) * BLOCK] for i in range(PAIRS_B)]
        return jnp.concatenate(rows + [jnp.zeros((16 - RESID, BLOCK), F32)], axis=0)

    def color_step(t, carry):
        pix = lanes_of(t, TILE_PIX)
        resid = jnp.concatenate([unpair(recv_b, tile_ref[l, t]) for l in range(LIST)], axis=1)
        looked = look_ref[t].astype(F32)
        eight = lax.broadcasted_iota(jnp.int32, (8, WIDTH), 0)
        palette = jnp.concatenate(
            [looked[:16] + resid, looked[16:], jnp.where(eight == 0, 0.5, 0.0)], axis=0
        ).astype(BF16)
        palette = nn(perm_ref[...], palette).astype(BF16)
        weight = wb_ref[pix, :]
        weight_lo = wl_ref[pix, :]
        mixed = nt(palette, weight) + nt(palette, weight_lo)
        harm = harm_ref[:, pix]
        image = [
            jnp.sum(harm * mixed[ch * 16 : (ch + 1) * 16], axis=0, keepdims=True) + mixed[48:49]
            for ch in range(3)
        ]
        for ch in range(3):
            img_ref[ch, :, pix] = image[ch]
        off = [image[ch] - target_ref[ch, :, pix].astype(F32) / 255.0 for ch in range(3)]
        total = off[0] + off[1] + off[2]
        pix8 = lax.broadcasted_iota(jnp.int32, (8, TILE_PIX), 0)
        grad = jnp.concatenate(
            [harm * off[ch] for ch in range(3)] + [jnp.where(pix8 == 0, total, 0.0)],
            axis=0,
        )
        grad_hi = grad.astype(BF16)
        grad_lo = (grad - grad_hi.astype(F32)).astype(BF16)
        both = jnp.concatenate([grad_hi, grad_lo], axis=0)
        both_ref[t] = both
        palette_ref[t] = jnp.concatenate([palette, palette], axis=0)
        color = nn(both, weight)
        color = color[:56] + color[56:] + nn(grad_hi, weight_lo)
        color_ref[t] = color.astype(BF16)
        for j in range(4):
            for ch in range(3):
                row = color[ch * 16 + j : ch * 16 + j + 1]
                for l in range(LIST):
                    grads_ref[pl.ds((3 * j + ch) * slots + l * tiles + t, 1), :] = row[
                        :, l * BLOCK : (l + 1) * BLOCK
                    ]
        return carry

    lane_d = lax.broadcasted_iota(jnp.int32, (1, n_space), 1)
    slot_hot = [
        jnp.where(lane_d == tile_ref[l, t], 1.0, 0.0) for l in range(LIST) for t in range(tiles)
    ]
    spot_ref[...] = jnp.concatenate(slot_hot * (n_space // slots), axis=0).T.astype(BF16)
    every_b = finish(msg_b, recv_b, 2)
    lax.fori_loop(0, tiles, color_step, 0, unroll=2)

    def to_slots(r, ref, row):
        part = grads_ref[r * slots : (r + 1) * slots, :]
        part_hi = part.astype(BF16).astype(F32)
        both = jnp.concatenate([part_hi, part - part_hi], axis=0).astype(BF16)
        put_rows(ref, row, nn(spot_ref[:, : 2 * slots], both))

    for r in range(RESID):
        to_slots(r, stage_ref, r)

    def fill_r(d):
        for i in range(PAIRS_B):
            msg_r[d, :, i * BLOCK : (i + 1) * BLOCK] = stage_ref[
                pl.ds(pl.multiple_of(d * STAGE, STAGE) + 2 * i, 2), :
            ].astype(BF16)

    to_space(n_space, fill_r, msg_r, recv_r, sems.at[4], sems.at[5])
    fill_r(me)
    recv_r[me] = msg_r[me]

    def word_step(t, carry):
        group = jnp.floor(message(t)[6:7] * 0.25)
        natural = tn(perm_ref[...], color_ref[t])[:COEF]
        masked = jnp.concatenate(
            [jnp.where(group == float(g), natural, 0.0).astype(BF16) for g in range(GROUPS)], axis=0
        )
        words_ref[...] += nt(masked, hot_ref[t])
        return carry

    lax.fori_loop(0, tiles, word_step, 0)
    for g in range(GROUPS):
        mine_ref[g] = words_ref[g * COEF : (g + 1) * COEF, :].astype(BF16)
    word_copies = around(
        lambda k: mine_ref.at[lax.rem(x + k, n_code)], lambda k: theirs_ref.at[k - 1], 3
    )

    def foot_step(t, carry):
        msg = message(t)
        cu, cv, ca, cb, cc, op = [msg[i : i + 1] for i in range(GEO)]
        du = u - cu
        g_ref[...] = tn(both_ref[t], palette_ref[t])
        for v in range(SIDE):
            rows = slice(v * SIDE, (v + 1) * SIDE)
            wg_ref[rows, :] = (wp_ref[v_rows(t, v), :] * g_ref[rows, :] * op).astype(BF16)
        cum_ref[:TILE_PIX, half:] = nn(wg_ref[:, half:], tris_ref[half:, half:])
        cum_ref[:TILE_PIX, :half] = nn(wg_ref[...], tris_ref[:, :half])
        s_zero = jnp.zeros((SIDE, WIDTH), F32)
        s_one = jnp.zeros((SIDE, WIDTH), F32)
        s_two = jnp.zeros((SIDE, WIDTH), F32)
        for v in range(SIDE):
            rows = slice(v * SIDE, (v + 1) * SIDE)
            e = e_ref[v_rows(t, v), :]
            p = wp_ref[v_rows(t, v), :] * g_ref[rows, :] - cum_ref[rows, :] * (
                e / (1.0 - op * e)
            )
            dv = (v - (SIDE - 1) * 0.5) - cv
            pd = p * dv
            s_zero = s_zero + p
            s_one = s_one + pd
            s_two = s_two + pd * dv
        m_zero = jnp.sum(s_zero, axis=0, keepdims=True)
        m_u = jnp.sum(s_zero * du, axis=0, keepdims=True)
        m_uu = jnp.sum(s_zero * du * du, axis=0, keepdims=True)
        m_v = jnp.sum(s_one, axis=0, keepdims=True)
        m_uv = jnp.sum(s_one * du, axis=0, keepdims=True)
        m_vv = jnp.sum(s_two, axis=0, keepdims=True)
        rows_back = [
            op * (ca * m_u + cb * m_v),
            op * (cb * m_u + cc * m_v),
            -0.5 * op * m_uu,
            -op * m_uv,
            -0.5 * op * m_vv,
            m_zero,
        ]
        for r, row in enumerate(rows_back):
            for l in range(LIST):
                grads_ref[pl.ds((RESID + r) * slots + l * tiles + t, 1), :] = row[
                    :, l * BLOCK : (l + 1) * BLOCK
                ]
        return carry

    lax.fori_loop(0, tiles, foot_step, 0)
    for copy in word_copies:
        copy.wait()
    total = words_ref[pl.ds(pl.multiple_of(x * COEF, COEF), COEF), :]
    for k in range(n_code - 1):
        total = total + theirs_ref[k].astype(F32)
    wide_ref[...] = nn(spread_ref[...], total.astype(BF16))
    planes, crowd = n_space // 8, 8
    plane, place = me // crowd, lax.rem(me, crowd)
    for j in range(planes):
        third = wide_ref[8 * j + 2 : 8 * j + 3, :]
        third = jnp.concatenate([third[:, : GWORDS // 2], third[:, GWORDS // 2 :]], axis=0)
        lines_out[j] = jnp.concatenate([wide_ref[8 * j : 8 * j + 2, :], third], axis=1).astype(BF16)

    def along(src, dst, first):
        copies = []
        for k in range(1, planes):
            there = lax.rem(plane + k, planes)
            copies.append(
                pltpu.make_async_remote_copy(
                    src_ref=src(there),
                    dst_ref=dst,
                    send_sem=far_send.at[first + k - 1],
                    recv_sem=far_recv.at[first + k - 1],
                    device_id={"space": there * crowd + place},
                    device_id_type=MESH,
                )
            )
            copies[-1].start()
        return copies

    line_copies = along(lambda there: lines_out.at[there], lines_in.at[plane], 0)
    lines_in[plane] = lines_out[plane]
    for r in range(GEO):
        to_slots(RESID + r, stage_t_ref, r)

    def fill_t(d):
        for i in range(PAIRS_T):
            msg_t[d, :, i * BLOCK : (i + 1) * BLOCK] = stage_t_ref[
                pl.ds(pl.multiple_of(d * STAGE, STAGE) + 2 * i, 2), :
            ].astype(BF16)

    to_space(n_space, fill_t, msg_t, recv_t, sems.at[6], sems.at[7])
    fill_t(me)
    recv_t[me] = msg_t[me]
    for copy in line_copies:
        copy.wait()
    total = lines_in[0].astype(F32)
    for j in range(1, planes):
        total = total + lines_in[j].astype(F32)
    near_ref[place] = total
    near = []
    for k in range(1, crowd):
        near.append(
            pltpu.make_async_remote_copy(
                src_ref=near_ref.at[place],
                dst_ref=near_ref.at[place],
                send_sem=near_send.at[k - 1],
                recv_sem=near_recv.at[k - 1],
                device_id={"space": plane * crowd + lax.rem(place + k, crowd)},
                device_id_type=MESH,
            )
        )
        near[-1].start()

    own_b = lax.broadcasted_iota(jnp.int32, (blocks, n_space), 0)
    own_hot = jnp.where(own_b == send_row_ref[...], 1.0, 0.0).astype(BF16)

    def spread_pairs(ref, stage, pairs):
        def one(d, carry):
            for i in range(pairs):
                stage[pl.ds(pl.multiple_of(d * STAGE, STAGE) + 2 * i, 2), :] = ref[
                    d, :, i * BLOCK : (i + 1) * BLOCK
                ].astype(F32)
            return carry

        lax.fori_loop(0, n_space, one, 0, unroll=4)

    def owned(stage, row):
        return nn(own_hot, get_rows(stage, row, n_space).astype(BF16))

    every_r = finish(msg_r, recv_r, 4)
    spread_pairs(recv_r, stage_ref, PAIRS_B)
    share = blocks // n_code
    chunk = RESID * share

    def chunk_of(i):
        return pl.ds(pl.multiple_of(i * chunk, chunk), chunk)

    for r in range(RESID):
        own = owned(stage_ref, r)
        for c in range(n_code):
            at = c * chunk + r * share
            own_resid_ref[at : at + share, :] = own[c * share : (c + 1) * share]
    resid_copies = around(
        lambda k: own_resid_ref.at[chunk_of(lax.rem(x + k, n_code))],
        lambda k: part_ref.at[k - 1],
        6,
    )
    for copy in near:
        copy.wait()
    total = near_ref[0]
    for k in range(1, crowd):
        total = total + near_ref[k]
    code_lines[plane] = total.astype(BF16)
    far = along(lambda there: code_lines.at[plane], code_lines.at[plane], planes - 1)
    for copy in resid_copies:
        copy.wait()
    total = own_resid_ref[chunk_of(x), :]
    for k in range(n_code - 1):
        total = total + part_ref[k]
    sum_ref[chunk_of(x), :] = total
    resid_copies = around(
        lambda k: sum_ref.at[chunk_of(x)],
        lambda k: sum_ref.at[chunk_of(x)],
        9,
    )

    every_t = finish(msg_t, recv_t, 6)
    spread_pairs(recv_t, stage_t_ref, PAIRS_T)
    for r in range(GEO):
        foot_ref[r] = owned(stage_t_ref, r)
    for copy in far:
        copy.wait()
    for j in range(planes):
        rows = code_lines[j].astype(F32)
        code_out_ref[3 * j : 3 * j + 2, :] = rows[:, :GWORDS]
        code_out_ref[3 * j + 2 : 3 * j + 3, : GWORDS // 2] = rows[0:1, GWORDS:]
        code_out_ref[3 * j + 2 : 3 * j + 3, GWORDS // 2 :] = rows[1:2, GWORDS:]
    for copy in resid_copies:
        copy.wait()
    for b in range(blocks):
        at = b // share * chunk + b % share
        resid_out_ref[:, b * BLOCK : (b + 1) * BLOCK] = sum_ref[pl.ds(at, RESID, stride=share), :]
    for every in (every_a, every_b, every_r, every_t):
        every.wait_send()


def hand_over_kernel(*refs):
    count = len(refs) // 2
    for i in range(count):
        refs[count + i][...] = refs[i][...]


def hand_over(arrays):
    return pl.pallas_call(
        hand_over_kernel,
        out_shape=tuple(jax.ShapeDtypeStruct(a.shape, a.dtype) for a in arrays),
        in_specs=[pl.BlockSpec(memory_space=pltpu.VMEM)] * len(arrays),
        out_specs=(pl.BlockSpec(memory_space=pltpu.VMEM),) * len(arrays),
        name="hand_over",
    )(*arrays)


def on_device(geometry, codebook, word_ids, residual, send_list, tile_list, rays, target):
    blocks = word_ids.shape[0] // BLOCK
    n_space = lax.axis_size("space")
    n_code = lax.axis_size("code")
    perm, spread = constants()
    tiles = tile_list.shape[1]
    pixels = rays.shape[2]
    splats = blocks * BLOCK
    sent = send_list[0, 0]
    vm = pltpu.VMEM
    dma = pltpu.SemaphoreType.DMA
    results = pl.pallas_call(
        functools.partial(step_kernel, n_space, n_code),
        out_shape=(
            jax.ShapeDtypeStruct((3, 1, pixels), F32),
            jax.ShapeDtypeStruct((GEO, blocks, BLOCK), F32),
            jax.ShapeDtypeStruct((RESID, splats), F32),
            jax.ShapeDtypeStruct((COEF, GWORDS), F32),
        ),
        in_specs=[pl.BlockSpec(memory_space=pltpu.SMEM)] * 2 + [pl.BlockSpec(memory_space=vm)] * 9,
        out_specs=(pl.BlockSpec(memory_space=vm),) * 4,
        scratch_shapes=[
            vm((blocks, 8, BLOCK), BF16),
            vm((blocks, 2, PAIRS_B * BLOCK), BF16),
            vm((n_space, 8, BLOCK), BF16),
            vm((n_space, 2, PAIRS_B * BLOCK), BF16),
            vm((n_space, 8, BLOCK), BF16),
            vm((n_space, 2, PAIRS_B * BLOCK), BF16),
            vm((n_code, COEF, GWORDS), BF16),
            vm((pixels, WIDTH), F32),
            vm((pixels, WIDTH), F32),
            vm((pixels, WIDTH), BF16),
            vm((pixels, WIDTH), BF16),
            vm((TILE_PIX, WIDTH), F32),
            vm((tiles, GWORDS, WIDTH), BF16),
            vm((tiles, COEF, WIDTH), BF16),
            vm((tiles, 56, WIDTH), BF16),
            vm((tiles, 112, TILE_PIX), BF16),
            vm((tiles, 112, WIDTH), BF16),
            vm((2 * TILE_PIX, WIDTH), BF16),
            vm((2 * TILE_PIX, WIDTH), F32),
            vm((TILE_PIX, WIDTH), BF16),
            vm((WIDTH, WIDTH), BF16),
            vm((WIDTH, WIDTH), BF16),
            vm((n_space, n_space), BF16),
            vm((16, pixels), F32),
            vm((GROUPS * COEF, GWORDS), F32),
            vm((n_code, COEF, GWORDS), BF16),
            vm((n_code - 1, COEF, GWORDS), BF16),
            vm((n_space, GWORDS), F32),
            vm(((RESID + GEO) * tiles * LIST, BLOCK), F32),
            vm((n_space * STAGE, BLOCK), F32),
            vm((n_space * STAGE, BLOCK), F32),
            vm((n_space, 2, PAIRS_B * BLOCK), BF16),
            vm((n_space, 2, PAIRS_B * BLOCK), BF16),
            vm((n_space, 2, PAIRS_T * BLOCK), BF16),
            vm((n_space, 2, PAIRS_T * BLOCK), BF16),
            vm((RESID * blocks, BLOCK), F32),
            vm((n_code - 1, RESID * blocks // n_code, BLOCK), F32),
            vm((RESID * blocks, BLOCK), F32),
            vm((n_space // 8, 2, 3 * GWORDS // 2), BF16),
            vm((n_space // 8, 2, 3 * GWORDS // 2), BF16),
            vm((8, 2, 3 * GWORDS // 2), F32),
            vm((n_space // 8, 2, 3 * GWORDS // 2), BF16),
            dma((8,)),
            dma((4 * (n_code - 1),)),
            dma((4 * (n_code - 1),)),
            dma((7,)),
            dma((7,)),
            dma((2 * (n_space // 8 - 1),)),
            dma((2 * (n_space // 8 - 1),)),
        ],
        compiler_params=pltpu.CompilerParams(
            collective_id=0, has_side_effects=True, vmem_limit_bytes=56 * 2**20
        ),
        name="step",
    )(
        sent,
        tile_list[0].T,
        sent.reshape(1, n_space),
        geometry[0],
        word_ids.reshape(blocks, BLOCK),
        residual,
        codebook,
        jnp.swapaxes(rays, 0, 1),
        jnp.swapaxes(target, 0, 1),
        perm,
        spread,
    )
    image, foot, resid_grad, code_grad = hand_over(results)
    image = jnp.swapaxes(image, 0, 1)
    foot = jnp.swapaxes(foot.reshape(GEO, 1, splats), 0, 1)
    return (image, foot, resid_grad, code_grad)


def solution(mesh):
    placed = (
        P("code", None, "space"),
        P(None, "code"),
        P("space"),
        P(None, "space"),
        P("code", "space", None),
        P("code", "space", None),
        P("code", None, "space"),
        P("code", None, "space"),
    )
    return jax.shard_map(
        on_device,
        mesh=mesh,
        in_specs=placed,
        out_specs=(
            P("code", None, "space"),
            P("code", None, "space"),
            P(None, "space"),
            P(None, "code"),
        ),
        check_vma=False,
    )
```
